256 devices in a mesh: sites: 64 (over z, y, core), rep: 4 (over x).
Axes of the slice: x: 4, y: 4, z: 8, core: 2. Of those that a mesh axis runs over, the one named last changes fastest.
Arguments:
- coords: float32 [2, 131072], P(None, 'sites'), may hold values from 0 to 53200, as said below
- scale: float32 [131072], P('sites'), may hold values from 0.5 to 2
- nugget: float32 [131072], P('sites'), may hold values from 0.2 to 1
- right_side: float32 [32, 131072], P(None, 'sites'), may hold values from -6 to 6
- site_order: int32 [131072], P('sites'), may hold values from 0 to 131071, as said below
- pair_list: int32 [2, 4608], P(None, ('sites', 'rep')), may hold values from 0 to 511, as said below
- pair_count: int32 [256], P(('sites', 'rep')), may hold values from 2 to 18, as said below
Outputs:
- solution_field: float32 [32, 131072], P(None, 'sites')
- residual: float32 [32, 131072], P(None, 'sites')
The draws below stay inside these ranges and needn't reach their ends.
Inputs may be any that keep to these rules, and one draw needn't show every extreme that they name: `site_order`: within the 2048 positions of each index of sites, a permutation of those same positions' indices. `pair_list`: each device's 18 slots hold its listed pairs first and (0, 0) after them. A listed pair has row <= column <= row + 8, column below 512, its row block among the 8 blocks of the device's index along sites; every pair of blocks with sites closer than 200 km is listed once, and no pair is listed twice. `pair_count`: every row block's own pair is listed; some devices list 18 pairs. `coords`: sites of block b lie in a band of east coordinates of its own; bands follow each other without gaps.
All inputs are finite; a program needn't handle non-finite values.
Results may differ from the reference program's by a relative error of at most 0.0003.
Values sent between devices are 32-bit elements; how exact they have to be, the bound alone decides.
A program may use at most 64 MiB of HBM per device.

```python
import math
import jax
import jax.numpy as jnp
from jax import lax

BLK = 256
RHS = 32
BPD = 8
ITERS = 3
SITES_DEV = 2048
NB = 512
NS = 131072
PSLOT = 18
PAIRS = 4608


def permute_group(group_key):
    return jax.random.permutation(group_key, SITES_DEV)


def strip_layout(key):
    width_key, group_key, order_key = jax.random.split(key, 3)
    least = 200 // BPD
    groups = NB // BPD
    widths = jax.random.randint(width_key, (NB,), least, 4 * least + 1, dtype=jnp.int32)
    dense_group = jax.random.randint(group_key, (), 0, groups - 1, dtype=jnp.int32)
    block_group = jnp.arange(NB, dtype=jnp.int32) // BPD
    forced = (block_group == dense_group) | (block_group == dense_group + 1)
    widths = jnp.where(forced, least, widths).astype(jnp.int32)
    starts = jnp.cumsum(widths) - widths
    order_keys = jax.random.split(order_key, groups)
    permuted = jax.vmap(permute_group)(order_keys).astype(jnp.int32)
    ordering = (permuted + jnp.arange(groups, dtype=jnp.int32)[:, None] * SITES_DEV).reshape(-1)
    return (widths, starts.astype(jnp.int32), ordering.astype(jnp.int32))


def pair_table(key):
    widths, starts, ordering = strip_layout(key)
    owners = PAIRS // PSLOT
    per_owner = PSLOT // (BPD + 1)
    row_block = jnp.arange(owners, dtype=jnp.int32)[:, None, None] * per_owner + jnp.arange(per_owner, dtype=jnp.int32)[None, :, None]
    col_block = row_block + jnp.arange(BPD + 1, dtype=jnp.int32)[None, None, :]
    row_block = jnp.broadcast_to(row_block, col_block.shape).reshape(owners, PSLOT)
    col_block = col_block.reshape(owners, PSLOT)
    band_end = jnp.take(starts + widths, row_block)
    spacing = jnp.take(starts, col_block, mode='clip') - band_end
    listed = (col_block < NB) & ((col_block == row_block) | (spacing < 200))
    scores = jnp.where(listed, 0, 1).astype(jnp.int32) * PSLOT + jnp.arange(PSLOT, dtype=jnp.int32)[None, :]
    ranked = jnp.argsort(scores, axis=1, stable=True)
    kept = jnp.take_along_axis(listed, ranked, 1)
    rows_sorted = jnp.where(kept, jnp.take_along_axis(row_block, ranked, 1), 0)
    cols_sorted = jnp.where(kept, jnp.take_along_axis(col_block, ranked, 1), 0)
    table = jnp.stack([rows_sorted.reshape(-1), cols_sorted.reshape(-1)]).astype(jnp.int32)
    counts = jnp.sum(listed.astype(jnp.int32), axis=1).astype(jnp.int32)
    return (table, counts)


def draw_site_order(key, part):
    return strip_layout(key)[2]


def draw_pair_list(key, part):
    return pair_table(key)[0]


def draw_pair_count(key, part):
    return pair_table(key)[1]


def draw_coords(key, part):
    widths, starts, ordering = strip_layout(key)
    key = jax.random.fold_in(key, 7)
    east_key, north_key = jax.random.split(key)
    block_of = jnp.arange(NS, dtype=jnp.int32) // BLK
    fraction = jax.random.uniform(east_key, (NS,), jnp.float32)
    span = 2000.0
    east = jnp.take(starts, block_of).astype(jnp.float32) + fraction * jnp.take(widths, block_of).astype(jnp.float32)
    north = jax.random.uniform(north_key, (NS,), jnp.float32) * span
    blocked = jnp.stack([east, north])
    return jnp.zeros((2, NS), jnp.float32).at[:, ordering].set(blocked)


def block_scale(own_key, shape, cuts, low, largest):
    loudness = 1.0
    for axis_at, parts in cuts:
        heights = jax.random.uniform(jax.random.fold_in(jax.random.fold_in(own_key, 6), axis_at), (parts,), jnp.float32, low / len(cuts), largest / len(cuts))
        loudness = loudness * jnp.repeat(jnp.exp(heights), shape[axis_at] // parts).reshape((-1,) + (1,) * (len(shape) - 1 - axis_at))
    return loudness


def gaussian(stream_key, dims, spread, limit, cuts=(), held_as=jnp.bfloat16):
    array = spread * jax.random.normal(stream_key, dims, jnp.float32)
    if cuts:
        array = array * block_scale(stream_key, dims, cuts, -0.22, 0.18)
    return jnp.clip(array, -limit, limit).astype(held_as)


def setup_inputs(seed: int = 0) -> dict:
    splits = jax.random.split(jax.random.key(seed), 8)
    coords = draw_coords(jax.random.fold_in(splits[7], 71), 0)
    scale = jnp.clip(jnp.exp(math.log(2.0) - 1.3862944 * jax.random.uniform(splits[1], (NS,), jnp.float32) ** block_scale(splits[1], (NS,), ((0, 64),), -0.2, 0.2)), 0.5, 2.0)
    nugget = jnp.clip(jnp.exp(math.log(1.0) - 1.609438 * jax.random.uniform(splits[2], (NS,), jnp.float32) ** block_scale(splits[2], (NS,), ((0, 64),), -0.2, 0.2)), 0.2, 1.0)
    right_side = gaussian(splits[3], (RHS, NS), 1.0, 6.0, ((1, 64),), jnp.float32)
    site_order = draw_site_order(jax.random.fold_in(splits[7], 71), 0)
    pair_list = draw_pair_list(jax.random.fold_in(splits[7], 71), 0)
    pair_count = draw_pair_count(jax.random.fold_in(splits[7], 71), 0)
    return dict(coords=coords, scale=scale, nugget=nugget, right_side=right_side, site_order=site_order, pair_list=pair_list, pair_count=pair_count)


RANGE_KM = 200.0
HIGHEST_PRECISION = lax.Precision.HIGHEST

def taper_tile(row_geo, col_geo):
    delta_east = row_geo[0][:, None] - col_geo[0][None, :]
    delta_north = row_geo[1][:, None] - col_geo[1][None, :]
    distance = jnp.sqrt(delta_east * delta_east + delta_north * delta_north)
    ratio = jnp.minimum(distance / RANGE_KM, 1.0)
    remain = 1.0 - ratio
    square = remain * remain
    return row_geo[2][:, None] * col_geo[2][None, :] * (square * square) * (1.0 + 4.0 * ratio)

def tile_terms(vectors, geo, row_start, col_start):
    tile = taper_tile(lax.dynamic_slice_in_dim(geo, row_start, BLK, 1), lax.dynamic_slice_in_dim(geo, col_start, BLK, 1))
    to_row = lax.dot_general(lax.dynamic_slice_in_dim(vectors, col_start, BLK, 1), tile, (((1,), (1,)), ((), ())), precision=HIGHEST_PRECISION, preferred_element_type=jnp.float32)
    to_col = jnp.dot(lax.dynamic_slice_in_dim(vectors, row_start, BLK, 1), tile, precision=HIGHEST_PRECISION, preferred_element_type=jnp.float32)
    return (to_row, to_col)

def add_block(accumulated, start, term):
    return lax.dynamic_update_slice_in_dim(accumulated, lax.dynamic_slice_in_dim(accumulated, start, BLK, 1) + term, start, 1)

def reference(coords, scale, nugget, right_side, site_order, pair_list, pair_count):
    geo = jnp.concatenate([coords[:, site_order], scale[site_order][None, :]], axis=0)
    damping = nugget[site_order]
    ordered = right_side[:, site_order]
    slot_ids = jnp.arange(PAIRS, dtype=jnp.int32)

    def operate(vectors):

        def add_pair(accumulated, slot):
            row_block = pair_list[0, slot]
            col_block = pair_list[1, slot]
            counted = slot % PSLOT < pair_count[slot // PSLOT]
            weight = jnp.where(counted, 1.0, 0.0).astype(vectors.dtype)
            distinct = jnp.where(row_block != col_block, weight, 0.0).astype(vectors.dtype)
            row_start = (row_block * BLK).astype(jnp.int32)
            col_start = (col_block * BLK).astype(jnp.int32)
            to_row, to_col = tile_terms(vectors, geo, row_start, col_start)
            accumulated = add_block(accumulated, row_start, to_row * weight)
            accumulated = add_block(accumulated, col_start, to_col * distinct)
            return (accumulated, None)
        accumulated, _ = lax.scan(add_pair, jnp.zeros_like(vectors), slot_ids)
        return accumulated + damping[None, :] * vectors
    solution = jnp.zeros_like(ordered)
    residual = ordered
    direction = ordered
    norm_now = lax.optimization_barrier(jnp.sum(residual * residual, axis=1))
    for iteration in range(ITERS):
        image = operate(direction)
        alpha = norm_now / lax.optimization_barrier(jnp.sum(direction * image, axis=1))
        solution = solution + alpha[:, None] * direction
        residual = residual - alpha[:, None] * image
        norm_next = lax.optimization_barrier(jnp.sum(residual * residual, axis=1))
        direction = residual + (norm_next / norm_now)[:, None] * direction
        norm_now = norm_next
    return (solution, residual)
```

```python
import functools

import jax
import jax.numpy as jnp
from jax import lax
from jax.experimental import pallas as pl
from jax.experimental.pallas import tpu as pltpu
from jax.sharding import PartitionSpec as P

MESH = pl.DeviceIdType.MESH
RANGE_KM = 200.0
TAPER_UNIT = 4.0 / RANGE_KM**5
F32 = jnp.float32
BF16 = jnp.bfloat16
REACH = 4
SLOTS = 2 * REACH + 1
OFFSETS = (1, -1, 2, -2, 3, -3, 4, -4)


def split3(value):
    high = value.astype(BF16).astype(F32)
    rest = value - high
    middle = rest.astype(BF16).astype(F32)
    return high, middle, rest - middle


def kernel(
    sizes,
    coords, scale, nugget, right_side, order,
    out_solution, out_residual,
    data, tile_high, tile_low, geo, halo, last, acc, sums1, sums2,
    geo_send, geo_recv, halo_send, halo_recv, last_send, last_recv,
    sum1_send, sum1_recv, sum2_send, sum2_recv,
):
    sites_n, rep_n, z_n, y_n = sizes
    group_width = right_side.shape[1]
    months = right_side.shape[0]
    width = group_width // rep_n
    chain_n = sites_n * rep_n
    my_s = lax.axis_index("sites")
    my_r = lax.axis_index("rep")
    chain = my_s * rep_n + my_r
    my_core = my_s % 2
    my_y = (my_s // 2) % y_n
    my_z = my_s // (2 * y_n)
    n1 = rep_n * y_n
    n2 = 2 * z_n
    place1 = my_r * y_n + my_y
    place2 = my_z * 2 + my_core

    def chain_device(offset):
        other = (chain + offset + chain_n) % chain_n
        return (other // rep_n, other % rep_n)

    def device1(step):
        other = (place1 + step) % n1
        return ((my_z * y_n + other % y_n) * 2 + my_core, other // y_n)

    def device2(step):
        other = (place2 + step) % n2
        return (((other // 2) * y_n + my_y) * 2 + other % 2, my_r)

    barrier = pltpu.get_barrier_semaphore()
    peers = (
        [chain_device(offset) for offset in OFFSETS]
        + [device1(step) for step in range(1, n1)]
        + [device2(step) for step in range(1, n2)]
    )
    for peer in peers:
        pl.semaphore_signal(barrier, inc=1, device_id=peer, device_id_type=MESH)

    site = jnp.concatenate(
        [coords[...], scale[...], nugget[...], jnp.zeros((4, group_width), F32)], axis=0
    )
    for at, part in enumerate(split3(right_side[...])):
        data[at * months:(at + 1) * months, :] = part.astype(BF16)
    parts = split3(site)
    top = 3 * months
    data[top:top + 16, :] = jnp.concatenate(parts[:2], axis=0).astype(BF16)
    data[top + 16:top + 32, :] = jnp.concatenate(
        [parts[2], jnp.zeros((8, group_width), F32)], axis=0
    ).astype(BF16)
    wanted = order[:, pl.ds(pl.multiple_of(my_r * width, width), width)] - my_s * group_width
    step_rows = 256
    rows_at = lax.broadcasted_iota(jnp.int32, (step_rows, width), 0)
    placed = jnp.zeros((top + 32, width), F32)
    for at in range(group_width // step_rows):
        chosen = jnp.where(rows_at == wanted - at * step_rows, 1.0, 0.0).astype(BF16)
        placed = placed + jnp.dot(
            data[:, at * step_rows:(at + 1) * step_rows], chosen, preferred_element_type=F32
        )
    ordered = (placed[:months] + placed[months:2 * months]) + placed[2 * months:top]
    own_geo = (placed[top:top + 8] + placed[top + 8:top + 16]) + placed[top + 16:top + 24]
    geo[REACH] = own_geo
    halo[0, REACH] = ordered

    pl.semaphore_wait(barrier, len(peers))

    def spread(source_of, send_sem, recv_of):
        for offset in OFFSETS:
            pltpu.make_async_remote_copy(
                src_ref=source_of(REACH), dst_ref=source_of(REACH - offset),
                send_sem=send_sem, recv_sem=recv_of(REACH - offset),
                device_id=chain_device(offset), device_id_type=MESH,
            ).start()

    def await_bytes(ref, sem):
        pltpu.make_async_copy(ref, ref, sem).wait()

    def spread_halo(stage):
        spread(lambda slot: halo.at[stage, slot], halo_send.at[stage], lambda slot: halo_recv.at[stage, slot])

    spread(lambda slot: geo.at[slot], geo_send, lambda slot: geo_recv.at[slot])
    spread_halo(0)

    own_scale = own_geo[2:3] * TAPER_UNIT
    own_nugget = own_geo[3:4]

    def make_tiles(slot):
        away = (chain + slot - REACH < 0) | (chain + slot - REACH >= chain_n)
        shift = jnp.where(away, 1.0e6, 0.0).astype(F32)
        columns = jnp.transpose(geo[slot])
        for at in range(0, width, step_rows):
            east = columns[at:at + step_rows, 0:1] + shift
            north = columns[at:at + step_rows, 1:2]
            d_east = east - own_geo[0:1]
            d_north = north - own_geo[1:2]
            squared = jnp.clip(d_east * d_east + d_north * d_north, 1.0e-30, RANGE_KM * RANGE_KM)
            distance = squared * lax.rsqrt(squared)
            remain = RANGE_KM - distance
            square = remain * remain
            tile = (square * square) * (distance + 0.25 * RANGE_KM)
            high = tile.astype(BF16)
            tile_high[slot, at:at + step_rows, :] = high
            tile_low[slot, at:at + step_rows, :] = (tile - high.astype(F32)).astype(BF16)

    def add_product(stage, slot):
        vector = halo[stage, slot] * geo[slot][2:3]
        high = vector.astype(BF16)
        low = (vector - high.astype(F32)).astype(BF16)
        both = jnp.dot(jnp.concatenate([high, low], axis=0), tile_high[slot], preferred_element_type=F32)
        small = jnp.dot(high, tile_low[slot], preferred_element_type=F32)
        acc[...] += both[:months] + (both[months:] + small)

    def slot_of(step):
        return REACH + (1 - 2 * (step % 2)) * ((step + 1) // 2) * -1

    def product(stage, midway, first):
        acc[...] = jnp.zeros_like(acc)
        if first:
            make_tiles(REACH)
        add_product(stage, REACH)

        def one(step, carry):
            slot = slot_of(step)
            if first:
                await_bytes(geo.at[slot], geo_recv.at[slot])
                make_tiles(slot)
            await_bytes(halo.at[stage, slot], halo_recv.at[stage, slot])
            add_product(stage, slot)
            return carry

        half = 5
        lax.fori_loop(1, half, one, 0)
        midway()
        lax.fori_loop(half, SLOTS, one, 0)
        return own_scale * acc[...] + own_nugget * halo[stage, REACH]

    def begin_sum(which, first, second):
        both = jnp.concatenate([first, second], axis=0)
        folded = both[:, :128]
        for at in range(128, width, 128):
            folded = folded + both[:, at:at + 128]
        folded = jnp.concatenate([folded, jnp.zeros((128 - 2 * months, 128), F32)], axis=0)
        sums1[which, place1] = jnp.sum(jnp.transpose(folded), axis=0, keepdims=True)
        for step in range(1, n1):
            pltpu.make_async_remote_copy(
                src_ref=sums1.at[which, place1], dst_ref=sums1.at[which, place1],
                send_sem=sum1_send.at[which], recv_sem=sum1_recv.at[which],
                device_id=device1(step), device_id_type=MESH,
            ).start()

    def pass_sum(which):
        await_bytes(sums1.at[which, pl.ds(0, n1 - 1)], sum1_recv.at[which])
        sums2[which, place2] = jnp.sum(sums1[which], axis=0)
        for step in range(1, n2):
            pltpu.make_async_remote_copy(
                src_ref=sums2.at[which, place2], dst_ref=sums2.at[which, place2],
                send_sem=sum2_send.at[which], recv_sem=sum2_recv.at[which],
                device_id=device2(step), device_id_type=MESH,
            ).start()

    def end_sum(which):
        await_bytes(sums2.at[which, pl.ds(0, n2 - 1)], sum2_recv.at[which])
        total = jnp.transpose(jnp.broadcast_to(jnp.sum(sums2[which], axis=0), (8, 128)))
        return total[:months, 0:1], total[months:2 * months, 0:1]

    image = product(0, lambda: None, True)
    halo[1, REACH] = image
    spread_halo(1)
    begin_sum(0, ordered * ordered, image * ordered)
    twice = product(1, lambda: pass_sum(0), False)
    norm0, curve0 = end_sum(0)
    alpha0 = norm0 / curve0
    residual1 = halo[0, REACH] - alpha0 * halo[1, REACH]
    image1 = halo[1, REACH] - alpha0 * twice
    halo[2, REACH] = image1
    spread_halo(2)
    begin_sum(1, residual1 * residual1, image1 * residual1)
    twice1 = product(2, lambda: pass_sum(1), False)
    last[my_r] = twice1
    for step in range(1, rep_n):
        pltpu.make_async_remote_copy(
            src_ref=last.at[my_r], dst_ref=last.at[my_r],
            send_sem=last_send, recv_sem=last_recv.at[step],
            device_id=(my_s, (my_r + step) % rep_n), device_id_type=MESH,
        ).start()
    norm1, curve1 = end_sum(1)
    beta1 = norm1 / norm0
    alpha1 = norm1 / (curve1 - beta1 * norm1 / alpha0)

    def second_step(place):
        slot = REACH + place - my_r
        start, first, second = halo[0, slot], halo[1, slot], halo[2, slot]
        before = start - alpha0 * first
        moved = second + beta1 * first
        direction = before + beta1 * start
        return (
            alpha0 * start + alpha1 * direction, before - alpha1 * moved, direction, moved,
            second - alpha1 * (last[place] + beta1 * ((first - second) / alpha0)),
        )

    _, residual2, _, _, image2 = second_step(my_r)
    begin_sum(2, residual2 * residual2, image2 * residual2)
    pass_sum(2)
    norm2, curve2 = end_sum(2)
    beta2 = norm2 / norm1
    alpha2 = norm2 / (curve2 - beta2 * norm2 / alpha1)
    for step in range(1, rep_n):
        await_bytes(last.at[0], last_recv.at[step])
    for place in range(rep_n):
        at = place * width
        found, residual, direction, moved, image2 = second_step(place)
        out_solution[:, at:at + width] = found + alpha2 * (residual + beta2 * direction)
        out_residual[:, at:at + width] = residual - alpha2 * (image2 + beta2 * moved)

    count = len(OFFSETS)
    await_bytes(geo.at[pl.ds(0, count)], geo_send)
    for stage in range(3):
        await_bytes(halo.at[stage, pl.ds(0, count)], halo_send.at[stage])
        await_bytes(sums1.at[stage, pl.ds(0, n1 - 1)], sum1_send.at[stage])
        await_bytes(sums2.at[stage, pl.ds(0, n2 - 1)], sum2_send.at[stage])
    await_bytes(last.at[pl.ds(0, rep_n - 1)], last_send)


def solution(mesh):
    sites_n, rep_n = mesh.shape["sites"], mesh.shape["rep"]
    y_n = 4
    z_n = sites_n // (2 * y_n)

    def local(coords, scale, nugget, right_side, site_order, pair_list, pair_count):
        months, group_width = right_side.shape
        width = group_width // rep_n
        vmem = pl.BlockSpec(memory_space=pltpu.VMEM)
        out = jax.ShapeDtypeStruct((months, group_width), F32)
        dma = pltpu.SemaphoreType.DMA
        return pl.pallas_call(
            functools.partial(kernel, (sites_n, rep_n, z_n, y_n)),
            out_shape=(out, out),
            in_specs=[vmem] * 5,
            out_specs=(vmem, vmem),
            scratch_shapes=[
                pltpu.VMEM((3 * months + 32, group_width), BF16),
                pltpu.VMEM((SLOTS, width, width), BF16),
                pltpu.VMEM((SLOTS, width, width), BF16),
                pltpu.VMEM((SLOTS, 8, width), F32),
                pltpu.VMEM((3, SLOTS, months, width), F32),
                pltpu.VMEM((rep_n, months, width), F32),
                pltpu.VMEM((months, width), F32),
                pltpu.VMEM((3, rep_n * y_n, 1, 128), F32),
                pltpu.VMEM((3, 2 * z_n, 1, 128), F32),
                dma, dma((SLOTS,)), dma((3,)), dma((3, SLOTS)), dma, dma((rep_n,)),
                dma((3,)), dma((3,)), dma((3,)), dma((3,)),
            ],
            compiler_params=pltpu.CompilerParams(
                collective_id=0, has_side_effects=True, vmem_limit_bytes=48 * 2**20
            ),
        )(coords, scale[None, :], nugget[None, :], right_side, site_order[None, :])

    in_specs = (
        P(None, "sites"),
        P("sites"),
        P("sites"),
        P(None, "sites"),
        P("sites"),
        P(None, ("sites", "rep")),
        P(("sites", "rep")),
    )
    out_specs = (P(None, "sites"), P(None, "sites"))
    return jax.shard_map(local, mesh=mesh, in_specs=in_specs, out_specs=out_specs, check_vma=False)
```

```python
import functools

import jax
import jax.numpy as jnp
from jax import lax
from jax.experimental import pallas as pl
from jax.experimental.pallas import tpu as pltpu
from jax.sharding import PartitionSpec as P

MESH = pl.DeviceIdType.MESH
RANGE_KM = 200.0
TAPER_UNIT = 4.0 / RANGE_KM**5
F32 = jnp.float32
BF16 = jnp.bfloat16
REACH = 4
SLOTS = 2 * REACH + 1
OFFSETS = (2, -2, 3, -3, 1, -1, 4, -4)


def split3(value):
    high = value.astype(BF16).astype(F32)
    rest = value - high
    middle = rest.astype(BF16).astype(F32)
    return high, middle, rest - middle


def kernel(
    sizes,
    coords_in, scale_in, nugget_in, right_side_in, order_in,
    out_powers, out_factors,
    coords, scale, nugget, right_side, order,
    data, tile_high, tile_low, geo, halo, last, acc, sums1, sums2,
    in_sems, out_sem, geo_send, geo_recv, halo_send, halo_recv, last_send, last_recv,
    sum1_send, sum1_recv, sum2_send, sum2_recv,
):
    sites_n, rep_n, z_n, y_n = sizes
    months, group_width = right_side.shape
    width = group_width // rep_n
    chain_n = sites_n * rep_n
    my_s = lax.axis_index("sites")
    my_r = lax.axis_index("rep")
    chain = my_s * rep_n + my_r
    my_core = my_s % 2
    my_y = (my_s // 2) % y_n
    my_z = my_s // (2 * y_n)
    n1 = rep_n * y_n
    n2 = 2 * z_n
    place1 = my_r * y_n + my_y
    place2 = my_z * 2 + my_core

    def chain_device(offset):
        other = (chain + offset + chain_n) % chain_n
        return (other // rep_n, other % rep_n)

    def device1(step):
        other = (place1 + step) % n1
        return ((my_z * y_n + other % y_n) * 2 + my_core, other // y_n)

    def device2(step):
        other = (place2 + step) % n2
        return (((other // 2) * y_n + my_y) * 2 + other % 2, my_r)

    barrier = pltpu.get_barrier_semaphore()
    peers = (
        [device2(step) for step in range(1, n2)]
        + [device1(step) for step in range(1, n1)]
        + [chain_device(offset) for offset in OFFSETS]
    )
    for peer in peers:
        pl.semaphore_signal(barrier, inc=1, device_id=peer, device_id_type=MESH)

    loads = [
        pltpu.make_async_copy(source, target, in_sems.at[at])
        for at, (source, target) in enumerate((
            (right_side_in, right_side), (coords_in, coords), (scale_in, scale),
            (nugget_in, nugget), (order_in, order),
        ))
    ]
    for load in loads:
        load.start()
    for load in loads:
        load.wait()

    def await_bytes(ref, sem):
        pltpu.make_async_copy(ref, ref, sem).wait()

    site = jnp.concatenate(
        [coords[...], scale[...], nugget[...], jnp.zeros((4, group_width), F32)], axis=0
    )
    for at, part in enumerate(split3(right_side[...])):
        data[at * months:(at + 1) * months, :] = part.astype(BF16)
    parts = split3(site)
    top = 3 * months
    data[top:top + 16, :] = jnp.concatenate(parts[:2], axis=0).astype(BF16)
    data[top + 16:top + 32, :] = jnp.concatenate(
        [parts[2], jnp.zeros((8, group_width), F32)], axis=0
    ).astype(BF16)
    step_rows = 256
    rows_at = lax.broadcasted_iota(jnp.int32, (step_rows, width), 0)

    def own_group_slot(turn):
        return REACH - my_r + (my_r + turn) % rep_n

    def place_sites(turn, carry):
        slot = own_group_slot(turn)
        start = pl.multiple_of(((my_r + turn) % rep_n) * width, width)
        wanted = order[:, pl.ds(start, width)] - my_s * group_width
        placed = jnp.zeros((top + 32, width), F32)
        for at in range(group_width // step_rows):
            chosen = jnp.where(rows_at == wanted - at * step_rows, 1.0, 0.0).astype(BF16)
            placed = placed + jnp.dot(
                data[:, at * step_rows:(at + 1) * step_rows], chosen, preferred_element_type=F32
            )
        halo[0, slot] = (placed[:months] + placed[months:2 * months]) + placed[2 * months:top]
        geo[slot] = (placed[top:top + 8] + placed[top + 8:top + 16]) + placed[top + 16:top + 24]
        return carry

    lax.fori_loop(0, rep_n, place_sites, 0)
    own_geo = geo[REACH]
    own_scale = own_geo[2:3] * TAPER_UNIT
    own_nugget = own_geo[3:4]

    def make_tiles(slot):
        away = (chain + slot - REACH < 0) | (chain + slot - REACH >= chain_n)
        shift = jnp.where(away, 1.0e6, 0.0).astype(F32)
        columns = jnp.transpose(geo[slot])
        for at in range(0, width, step_rows):
            east = columns[at:at + step_rows, 0:1] + shift
            north = columns[at:at + step_rows, 1:2]
            d_east = east - own_geo[0:1]
            d_north = north - own_geo[1:2]
            squared = jnp.clip(d_east * d_east + d_north * d_north, 1.0e-30, RANGE_KM * RANGE_KM)
            distance = squared * lax.rsqrt(squared)
            remain = RANGE_KM - distance
            square = remain * remain
            tile = (square * square) * (distance + 0.25 * RANGE_KM)
            high = tile.astype(BF16)
            tile_high[slot, at:at + step_rows, :] = high
            tile_low[slot, at:at + step_rows, :] = (tile - high.astype(F32)).astype(BF16)

    def add_product(stage, slot):
        vector = halo[stage, slot] * geo[slot][2:3]
        high = vector.astype(BF16)
        low = (vector - high.astype(F32)).astype(BF16)
        both = jnp.dot(jnp.concatenate([high, low], axis=0), tile_high[slot], preferred_element_type=F32)
        small = jnp.dot(high, tile_low[slot], preferred_element_type=F32)
        acc[...] += both[:months] + (both[months:] + small)

    def image_of(stage):
        return own_scale * acc[...] + own_nugget * halo[stage, REACH]

    acc[...] = jnp.zeros_like(acc)

    def own_tiles(turn, carry):
        make_tiles(own_group_slot(turn))
        return carry

    lax.fori_loop(0, rep_n, own_tiles, 0)

    pl.semaphore_wait(barrier, len(peers))

    def upward(turn):
        return turn <= rep_n - 1 - my_r

    def exchange(ref_of, send_sem, recv_of):
        for turn in range(rep_n + 1):
            up = upward(turn)
            source = jnp.where(up, REACH + turn, turn)
            target = jnp.where(up, turn, REACH + turn)
            group = (my_s + jnp.where(up, 1, sites_n - 1)) % sites_n
            pltpu.make_async_remote_copy(
                src_ref=ref_of(source), dst_ref=ref_of(target), send_sem=send_sem, recv_sem=recv_of(target),
                device_id=(group, my_r), device_id_type=MESH,
            ).start()

    exchange(lambda slot: geo.at[slot], geo_send, lambda slot: geo_recv.at[slot])
    exchange(lambda slot: halo.at[0, slot], halo_send.at[0], lambda slot: halo_recv.at[0, slot])

    def own_products(turn, carry):
        add_product(0, own_group_slot(turn))
        return carry

    lax.fori_loop(0, rep_n, own_products, 0)

    def come_slot(turn):
        return jnp.where(upward(turn), turn, REACH + turn)

    def other_tiles(turn, carry):
        slot = come_slot(turn)
        await_bytes(geo.at[slot], geo_recv.at[slot])
        make_tiles(slot)
        return carry

    lax.fori_loop(0, rep_n + 1, other_tiles, 0)

    def other_products(turn, carry):
        slot = come_slot(turn)
        await_bytes(halo.at[0, slot], halo_recv.at[0, slot])
        add_product(0, slot)
        return carry

    lax.fori_loop(0, rep_n + 1, other_products, 0)

    def spread_halo(stage):
        for offset in OFFSETS:
            pltpu.make_async_remote_copy(
                src_ref=halo.at[stage, REACH], dst_ref=halo.at[stage, REACH - offset],
                send_sem=halo_send.at[stage], recv_sem=halo_recv.at[stage, REACH - offset],
                device_id=chain_device(offset), device_id_type=MESH,
            ).start()

    def write_power(power, source_of):
        for place in range(rep_n):
            pltpu.make_async_copy(
                source_of(place), out_powers.at[power, :, place * width:(place + 1) * width], out_sem
            ).start()

    def write_halo(stage):
        write_power(stage, lambda place: halo.at[stage, REACH + place - my_r])

    def product(stage):
        acc[...] = jnp.zeros_like(acc)
        add_product(stage, REACH)

        def one(step, carry):
            reach = jnp.where(step < 2, 4, jnp.where(step < 4, 1, jnp.where(step < 6, 3, 2)))
            slot = REACH + (1 - 2 * (step % 2)) * reach
            await_bytes(halo.at[stage, slot], halo_recv.at[stage, slot])
            add_product(stage, slot)
            return carry

        lax.fori_loop(0, 2 * REACH, one, 0)
        return image_of(stage)

    def folded(first, second):
        value = first * second
        total = value[:, :128]
        for at in range(128, width, 128):
            total = total + value[:, at:at + 128]
        return total

    def as_row(pieces):
        return jnp.sum(jnp.transpose(jnp.concatenate(pieces, axis=0)), axis=0, keepdims=True)

    halo[1, REACH] = image_of(0)
    spread_halo(1)
    write_halo(0)
    halo[2, REACH] = product(1)
    spread_halo(2)
    write_halo(1)
    start, first, second = halo[0, REACH], halo[1, REACH], halo[2, REACH]
    sums1[place1, 0:1] = as_row(
        [folded(start, start), folded(start, first), folded(first, first), folded(first, second)]
    )
    square2 = folded(second, second)
    third = product(2)
    sums1[place1, 1:2] = as_row(
        [square2, folded(halo[2, REACH], third), jnp.zeros((128 - 2 * months, 128), F32)]
    )
    for step in range(1, n1):
        pltpu.make_async_remote_copy(
            src_ref=sums1.at[place1], dst_ref=sums1.at[place1], send_sem=sum1_send, recv_sem=sum1_recv,
            device_id=device1(step), device_id_type=MESH,
        ).start()
    last[my_r] = third
    for step in range(1, rep_n):
        pltpu.make_async_remote_copy(
            src_ref=last.at[my_r], dst_ref=last.at[my_r],
            send_sem=last_send, recv_sem=last_recv.at[step],
            device_id=(my_s, (my_r + step) % rep_n), device_id_type=MESH,
        ).start()
    write_halo(2)
    await_bytes(sums1.at[pl.ds(0, n1 - 1)], sum1_recv)
    sums2[place2] = jnp.sum(sums1[...], axis=0)
    for step in range(1, n2):
        pltpu.make_async_remote_copy(
            src_ref=sums2.at[place2], dst_ref=sums2.at[place2], send_sem=sum2_send, recv_sem=sum2_recv,
            device_id=device2(step), device_id_type=MESH,
        ).start()
    for step in range(1, rep_n):
        await_bytes(last.at[0], last_recv.at[step])
    write_power(3, lambda place: last.at[place])
    count = len(OFFSETS)
    await_bytes(geo.at[pl.ds(0, rep_n + 1)], geo_send)
    await_bytes(halo.at[0, pl.ds(0, rep_n + 1)], halo_send.at[0])
    for stage in range(1, 3):
        await_bytes(halo.at[stage, pl.ds(0, count)], halo_send.at[stage])
    await_bytes(last.at[pl.ds(0, rep_n - 1)], last_send)
    await_bytes(sums1.at[pl.ds(0, n1 - 1)], sum1_send)
    await_bytes(out_powers, out_sem)

    await_bytes(sums2.at[pl.ds(0, n2 - 1)], sum2_recv)
    rows = jnp.sum(sums2[...], axis=0)
    total = jnp.transpose(jnp.concatenate([rows, jnp.zeros((6, 128), F32)], axis=0))
    m0, m1, m2, m3 = [total[at * months:(at + 1) * months, 0:1] for at in range(4)]
    m4, m5 = [total[at * months:(at + 1) * months, 1:2] for at in range(2)]
    alpha0 = m0 / m1
    norm1 = m0 - 2.0 * alpha0 * m1 + alpha0 * alpha0 * m2
    lead = 1.0 + norm1 / m0
    alpha1 = norm1 / (lead * lead * m1 - 2.0 * lead * alpha0 * m2 + alpha0 * alpha0 * m3)
    r1 = -(alpha0 + alpha1 * lead)
    r2 = alpha0 * alpha1
    norm2 = m0 + 2.0 * r1 * m1 + (r1 * r1 + 2.0 * r2) * m2 + 2.0 * r1 * r2 * m3 + r2 * r2 * m4
    beta2 = norm2 / norm1
    d0 = 1.0 + beta2 * lead
    d1 = r1 - beta2 * alpha0
    alpha2 = norm2 / (
        d0 * d0 * m1 + 2.0 * d0 * d1 * m2 + (d1 * d1 + 2.0 * d0 * r2) * m3 + 2.0 * d1 * r2 * m4 + r2 * r2 * m5
    )
    factors = (
        alpha0 + alpha1 * lead + alpha2 * d0, alpha2 * d1 - alpha1 * alpha0, alpha2 * r2,
        r1 - alpha2 * d0, r2 - alpha2 * d1, -alpha2 * r2,
    )
    lanes = lax.broadcasted_iota(jnp.int32, (months, 128), 1)
    table = jnp.zeros((months, 128), F32)
    for at, factor in enumerate(factors):
        table = jnp.where(lanes == at, factor, table)
    out_factors[...] = table
    await_bytes(sums2.at[pl.ds(0, n2 - 1)], sum2_send)


def solution(mesh):
    sites_n, rep_n = mesh.shape["sites"], mesh.shape["rep"]
    y_n = 4
    z_n = sites_n // (2 * y_n)

    def local(coords, scale, nugget, right_side, site_order, pair_list, pair_count):
        months, group_width = right_side.shape
        width = group_width // rep_n
        anywhere = pl.BlockSpec(memory_space=pl.ANY)
        vmem = pl.BlockSpec(memory_space=pltpu.VMEM)
        dma = pltpu.SemaphoreType.DMA
        powers, factors = pl.pallas_call(
            functools.partial(kernel, (sites_n, rep_n, z_n, y_n)),
            out_shape=(
                jax.ShapeDtypeStruct((4, months, group_width), F32), jax.ShapeDtypeStruct((months, 128), F32)
            ),
            in_specs=[anywhere] * 5,
            out_specs=(anywhere, vmem),
            scratch_shapes=[
                pltpu.VMEM((2, group_width), F32),
                pltpu.VMEM((1, group_width), F32),
                pltpu.VMEM((1, group_width), F32),
                pltpu.VMEM((months, group_width), F32),
                pltpu.VMEM((1, group_width), jnp.int32),
                pltpu.VMEM((3 * months + 32, group_width), BF16),
                pltpu.VMEM((SLOTS, width, width), BF16),
                pltpu.VMEM((SLOTS, width, width), BF16),
                pltpu.VMEM((SLOTS, 8, width), F32),
                pltpu.VMEM((3, SLOTS, months, width), F32),
                pltpu.VMEM((rep_n, months, width), F32),
                pltpu.VMEM((months, width), F32),
                pltpu.VMEM((rep_n * y_n, 2, 128), F32),
                pltpu.VMEM((2 * z_n, 2, 128), F32),
                dma((5,)), dma, dma, dma((SLOTS,)), dma((3,)), dma((3, SLOTS)), dma, dma((rep_n,)),
                dma, dma, dma, dma,
            ],
            compiler_params=pltpu.CompilerParams(
                collective_id=0, has_side_effects=True, vmem_limit_bytes=56 * 2**20
            ),
        )(coords, scale[None, :], nugget[None, :], right_side, site_order[None, :])
        part = [factors[:, at:at + 1] for at in range(6)]
        found = part[0] * powers[0] + part[1] * powers[1] + part[2] * powers[2]
        residual = powers[0] + part[3] * powers[1] + part[4] * powers[2] + part[5] * powers[3]
        return (found, residual)

    in_specs = (
        P(None, "sites"),
        P("sites"),
        P("sites"),
        P(None, "sites"),
        P("sites"),
        P(None, ("sites", "rep")),
        P(("sites", "rep")),
    )
    out_specs = (P(None, "sites"), P(None, "sites"))
    return jax.shard_map(local, mesh=mesh, in_specs=in_specs, out_specs=out_specs, check_vma=False)
```

```python
import functools

import jax
import jax.numpy as jnp
from jax import lax
from jax.experimental import pallas as pl
from jax.experimental.pallas import tpu as pltpu
from jax.sharding import PartitionSpec as P

MESH = pl.DeviceIdType.MESH
RANGE_KM = 200.0
TAPER_UNIT = 4.0 / RANGE_KM**5
F32 = jnp.float32
BF16 = jnp.bfloat16
REACH = 4
SLOTS = 2 * REACH + 1
AHEAD = (-2, -3, -1, -4)
BEHIND = (2, 3, 1, 4)
OFFSETS = AHEAD + BEHIND


def split3(value):
    high = value.astype(BF16).astype(F32)
    rest = value - high
    middle = rest.astype(BF16).astype(F32)
    return high, middle, rest - middle


def kernel(
    sizes,
    coords_in, scale_in, nugget_in, right_side_in, order_in,
    out_powers, out_factors,
    coords, scale, nugget, right_side, order,
    data, tile_high, tile_low, geo, halo, last, acc, sums1, sums2,
    in_sems, out_sem, geo_send, geo_recv, halo_send, halo_recv, last_send, last_recv,
    sum1_send, sum1_recv, sum2_send, sum2_recv,
):
    sites_n, rep_n, z_n, y_n = sizes
    months, group_width = right_side.shape
    width = group_width // rep_n
    chain_n = sites_n * rep_n
    my_s = lax.axis_index("sites")
    my_r = lax.axis_index("rep")
    chain = my_s * rep_n + my_r
    my_core = my_s % 2
    my_y = (my_s // 2) % y_n
    my_z = my_s // (2 * y_n)
    n1 = rep_n * y_n
    n2 = 2 * z_n
    place1 = my_r * y_n + my_y
    place2 = my_z * 2 + my_core

    def chain_device(offset):
        other = (chain + offset + chain_n) % chain_n
        return (other // rep_n, other % rep_n)

    def device1(step):
        other = (place1 + step) % n1
        return ((my_z * y_n + other % y_n) * 2 + my_core, other // y_n)

    def device2(step):
        other = (place2 + step) % n2
        return (((other // 2) * y_n + my_y) * 2 + other % 2, my_r)

    barrier = pltpu.get_barrier_semaphore()
    peers = (
        [device2(step) for step in range(1, n2)]
        + [device1(step) for step in range(1, n1)]
        + [chain_device(offset) for offset in OFFSETS]
    )
    for peer in peers:
        pl.semaphore_signal(barrier, inc=1, device_id=peer, device_id_type=MESH)

    loads = [
        pltpu.make_async_copy(source, target, in_sems.at[at])
        for at, (source, target) in enumerate((
            (right_side_in, right_side), (coords_in, coords), (scale_in, scale),
            (nugget_in, nugget), (order_in, order),
        ))
    ]
    for load in loads:
        load.start()
    for load in loads:
        load.wait()

    def await_bytes(ref, sem):
        pltpu.make_async_copy(ref, ref, sem).wait()

    site = jnp.concatenate(
        [coords[...], scale[...], nugget[...], jnp.zeros((4, group_width), F32)], axis=0
    )
    for at, part in enumerate(split3(right_side[...])):
        data[at * months:(at + 1) * months, :] = part.astype(BF16)
    parts = split3(site)
    top = 3 * months
    data[top:top + 16, :] = jnp.concatenate(parts[:2], axis=0).astype(BF16)
    data[top + 16:top + 32, :] = jnp.concatenate(
        [parts[2], jnp.zeros((8, group_width), F32)], axis=0
    ).astype(BF16)
    step_rows = 256
    rows_at = lax.broadcasted_iota(jnp.int32, (step_rows, width), 0)

    def own_group_slot(turn):
        return REACH - my_r + (my_r + turn) % rep_n

    def place_sites(turn, carry):
        slot = own_group_slot(turn)
        start = pl.multiple_of(((my_r + turn) % rep_n) * width, width)
        wanted = order[:, pl.ds(start, width)] - my_s * group_width
        placed = jnp.zeros((top + 32, width), F32)
        for at in range(group_width // step_rows):
            chosen = jnp.where(rows_at == wanted - at * step_rows, 1.0, 0.0).astype(BF16)
            placed = placed + jnp.dot(
                data[:, at * step_rows:(at + 1) * step_rows], chosen, preferred_element_type=F32
            )
        halo[0, slot] = (placed[:months] + placed[months:2 * months]) + placed[2 * months:top]
        geo[slot] = (placed[top:top + 8] + placed[top + 8:top + 16]) + placed[top + 16:top + 24]
        return carry

    lax.fori_loop(0, rep_n, place_sites, 0)
    own_geo = geo[REACH]
    own_scale = own_geo[2:3] * TAPER_UNIT
    own_nugget = own_geo[3:4]

    def split2(vector):
        high = vector.astype(BF16)
        return high, (vector - high.astype(F32)).astype(BF16)

    def make_tiles(slot):
        away = (chain + slot - REACH < 0) | (chain + slot - REACH >= chain_n)
        shift = jnp.where(away, 1.0e6, 0.0).astype(F32)
        columns = jnp.transpose(geo[slot])

        def chunk(at):
            east = columns[at:at + step_rows, 0:1] + shift
            north = columns[at:at + step_rows, 1:2]
            d_east = east - own_geo[0:1]
            d_north = north - own_geo[1:2]
            squared = jnp.clip(d_east * d_east + d_north * d_north, 1.0e-30, RANGE_KM * RANGE_KM)
            distance = squared * lax.rsqrt(squared)
            remain = RANGE_KM - distance
            square = remain * remain
            high, low = split2((square * square) * (distance + 0.25 * RANGE_KM))
            tile_high[slot, at:at + step_rows, :] = high
            tile_low[slot, at:at + step_rows, :] = low

        for at in range(0, width, step_rows):
            chunk(at)

    def add_product(stage, slot):
        vector = halo[stage, slot] * geo[slot][2:3]
        high, low = split2(vector)
        both = jnp.dot(jnp.concatenate([high, low], axis=0), tile_high[slot], preferred_element_type=F32)
        small = jnp.dot(high, tile_low[slot], preferred_element_type=F32)
        acc[...] += both[:months] + (both[months:] + small)

    def image_of(stage):
        return own_scale * acc[...] + own_nugget * halo[stage, REACH]

    pl.semaphore_wait(barrier, len(peers))

    def upward(turn):
        return turn <= rep_n - 1 - my_r

    def exchange(ref_of, send_sem, recv_of):
        for turn in range(rep_n + 1):
            up = upward(turn)
            source = jnp.where(up, REACH + turn, turn)
            target = jnp.where(up, turn, REACH + turn)
            group = (my_s + jnp.where(up, 1, sites_n - 1)) % sites_n
            pltpu.make_async_remote_copy(
                src_ref=ref_of(source), dst_ref=ref_of(target), send_sem=send_sem, recv_sem=recv_of(target),
                device_id=(group, my_r), device_id_type=MESH,
            ).start()

    exchange(lambda slot: geo.at[slot], geo_send, lambda slot: geo_recv.at[slot])
    exchange(lambda slot: halo.at[0, slot], halo_send.at[0], lambda slot: halo_recv.at[0, slot])

    acc[...] = jnp.zeros_like(acc)

    def own_pieces(turn, carry):
        slot = own_group_slot(turn)
        make_tiles(slot)
        add_product(0, slot)
        return carry

    lax.fori_loop(0, rep_n, own_pieces, 0)

    def other_pieces(turn, carry):
        slot = jnp.where(upward(turn), turn, REACH + turn)
        await_bytes(geo.at[slot], geo_recv.at[slot])
        make_tiles(slot)
        await_bytes(halo.at[0, slot], halo_recv.at[0, slot])
        add_product(0, slot)
        return carry

    lax.fori_loop(0, rep_n + 1, other_pieces, 0)

    def spread_halo(stage):
        for offset in OFFSETS:
            pltpu.make_async_remote_copy(
                src_ref=halo.at[stage, REACH], dst_ref=halo.at[stage, REACH - offset],
                send_sem=halo_send.at[stage], recv_sem=halo_recv.at[stage, REACH - offset],
                device_id=chain_device(offset), device_id_type=MESH,
            ).start()

    def write_power(power, source_of):
        for place in range(rep_n):
            pltpu.make_async_copy(
                source_of(place), out_powers.at[power, :, place * width:(place + 1) * width], out_sem
            ).start()

    def write_halo(stage):
        write_power(stage, lambda place: halo.at[stage, REACH + place - my_r])

    def add_side(stage, sign):
        def one(step, carry):
            reach = jnp.where(step == 0, 4, jnp.where(step == 1, 1, jnp.where(step == 2, 3, 2)))
            slot = REACH + sign * reach
            await_bytes(halo.at[stage, slot], halo_recv.at[stage, slot])
            add_product(stage, slot)
            return carry

        lax.fori_loop(0, REACH, one, 0)

    def folded(first, second):
        value = first * second
        total = value[:, :128]
        for at in range(128, width, 128):
            total = total + value[:, at:at + 128]
        return total

    def as_row(pieces):
        return jnp.sum(jnp.transpose(jnp.concatenate(pieces, axis=0)), axis=0, keepdims=True)

    halo[1, REACH] = image_of(0)
    spread_halo(1)
    write_halo(0)
    acc[...] = jnp.zeros_like(acc)
    add_product(1, REACH)
    add_side(1, 1)
    add_side(1, -1)
    halo[2, REACH] = image_of(1)
    spread_halo(2)
    write_halo(1)
    start, first, second = halo[0, REACH], halo[1, REACH], halo[2, REACH]
    sums1[place1, 0:1] = as_row(
        [folded(start, start), folded(start, first), folded(first, first), folded(first, second)]
    )
    square2 = folded(second, second)
    acc[...] = jnp.zeros_like(acc)
    add_product(2, REACH)
    within = acc[...]
    add_side(2, 1)
    doubled = own_scale * (2.0 * acc[...] - within) + own_nugget * halo[2, REACH]
    sums1[place1, 1:2] = as_row(
        [square2, folded(halo[2, REACH], doubled), jnp.zeros((128 - 2 * months, 128), F32)]
    )
    for step in range(1, n1):
        pltpu.make_async_remote_copy(
            src_ref=sums1.at[place1], dst_ref=sums1.at[place1], send_sem=sum1_send, recv_sem=sum1_recv,
            device_id=device1(step), device_id_type=MESH,
        ).start()
    add_side(2, -1)
    last[my_r] = image_of(2)
    for step in range(1, rep_n):
        pltpu.make_async_remote_copy(
            src_ref=last.at[my_r], dst_ref=last.at[my_r],
            send_sem=last_send, recv_sem=last_recv.at[step],
            device_id=(my_s, (my_r + step) % rep_n), device_id_type=MESH,
        ).start()
    write_halo(2)
    await_bytes(sums1.at[pl.ds(0, n1 - 1)], sum1_recv)
    sums2[place2] = jnp.sum(sums1[...], axis=0)
    for step in range(1, n2):
        pltpu.make_async_remote_copy(
            src_ref=sums2.at[place2], dst_ref=sums2.at[place2], send_sem=sum2_send, recv_sem=sum2_recv,
            device_id=device2(step), device_id_type=MESH,
        ).start()
    for step in range(1, rep_n):
        await_bytes(last.at[0], last_recv.at[step])
    write_power(3, lambda place: last.at[place])
    count = len(OFFSETS)
    await_bytes(geo.at[pl.ds(0, rep_n + 1)], geo_send)
    await_bytes(halo.at[0, pl.ds(0, rep_n + 1)], halo_send.at[0])
    for stage in range(1, 3):
        await_bytes(halo.at[stage, pl.ds(0, count)], halo_send.at[stage])
    await_bytes(last.at[pl.ds(0, rep_n - 1)], last_send)
    await_bytes(sums1.at[pl.ds(0, n1 - 1)], sum1_send)
    await_bytes(out_powers, out_sem)

    await_bytes(sums2.at[pl.ds(0, n2 - 1)], sum2_recv)
    rows = jnp.sum(sums2[...], axis=0)
    total = jnp.transpose(jnp.concatenate([rows, jnp.zeros((6, 128), F32)], axis=0))
    m0, m1, m2, m3 = [total[at * months:(at + 1) * months, 0:1] for at in range(4)]
    m4, m5 = [total[at * months:(at + 1) * months, 1:2] for at in range(2)]
    alpha0 = m0 / m1
    norm1 = alpha0 * alpha0 * m2 - m0
    lead = 1.0 + norm1 / m0
    alpha1 = norm1 / (alpha0 * (alpha0 * m3 - lead * m2))
    r1 = -(alpha0 + alpha1 * lead)
    r2 = alpha0 * alpha1
    norm2 = r2 * (m2 + r1 * m3 + r2 * m4)
    beta2 = norm2 / norm1
    d0 = 1.0 + beta2 * lead
    d1 = r1 - beta2 * alpha0
    alpha2 = norm2 / (r2 * (d0 * m3 + d1 * m4 + r2 * m5))
    factors = (
        alpha0 + alpha1 * lead + alpha2 * d0, alpha2 * d1 - alpha1 * alpha0, alpha2 * r2,
        r1 - alpha2 * d0, r2 - alpha2 * d1, -alpha2 * r2,
    )
    lanes = lax.broadcasted_iota(jnp.int32, (months, 128), 1)
    table = jnp.zeros((months, 128), F32)
    for at, factor in enumerate(factors):
        table = jnp.where(lanes == at, factor, table)
    out_factors[...] = table
    await_bytes(sums2.at[pl.ds(0, n2 - 1)], sum2_send)


def combine(powers, factors, out_solution, out_residual, held, made, in_sems, out_sems):
    parts = in_sems.shape[0]
    width = held.shape[2] // parts
    loads, stores = [], []
    for at in range(parts):
        lanes = slice(at * width, (at + 1) * width)
        load = pltpu.make_async_copy(powers.at[:, :, lanes], held.at[:, :, lanes], in_sems.at[at])
        load.start()
        loads.append(load)
    part = [factors[:, at:at + 1] for at in range(6)]
    for at in range(parts):
        lanes = slice(at * width, (at + 1) * width)
        loads[at].wait()
        start, first, second, third = (held[power, :, lanes] for power in range(4))
        made[0, :, lanes] = part[0] * start + part[1] * first + part[2] * second
        made[1, :, lanes] = start + part[3] * first + part[4] * second + part[5] * third
        for which, out in enumerate((out_solution, out_residual)):
            store = pltpu.make_async_copy(made.at[which, :, lanes], out.at[:, lanes], out_sems.at[which, at])
            store.start()
            stores.append(store)
    for store in stores:
        store.wait()


def solution(mesh):
    sites_n, rep_n = mesh.shape["sites"], mesh.shape["rep"]
    y_n = 4
    z_n = sites_n // (2 * y_n)

    def local(coords, scale, nugget, right_side, site_order, pair_list, pair_count):
        months, group_width = right_side.shape
        width = group_width // rep_n
        anywhere = pl.BlockSpec(memory_space=pl.ANY)
        vmem = pl.BlockSpec(memory_space=pltpu.VMEM)
        dma = pltpu.SemaphoreType.DMA
        powers, factors = pl.pallas_call(
            functools.partial(kernel, (sites_n, rep_n, z_n, y_n)),
            out_shape=(
                jax.ShapeDtypeStruct((4, months, group_width), F32), jax.ShapeDtypeStruct((months, 128), F32)
            ),
            in_specs=[anywhere] * 5,
            out_specs=(anywhere, vmem),
            scratch_shapes=[
                pltpu.VMEM((2, group_width), F32),
                pltpu.VMEM((1, group_width), F32),
                pltpu.VMEM((1, group_width), F32),
                pltpu.VMEM((months, group_width), F32),
                pltpu.VMEM((1, group_width), jnp.int32),
                pltpu.VMEM((3 * months + 32, group_width), BF16),
                pltpu.VMEM((SLOTS, width, width), BF16),
                pltpu.VMEM((SLOTS, width, width), BF16),
                pltpu.VMEM((SLOTS, 8, width), F32),
                pltpu.VMEM((3, SLOTS, months, width), F32),
                pltpu.VMEM((rep_n, months, width), F32),
                pltpu.VMEM((months, width), F32),
                pltpu.VMEM((rep_n * y_n, 2, 128), F32),
                pltpu.VMEM((2 * z_n, 2, 128), F32),
                dma((5,)), dma, dma, dma((SLOTS,)), dma((3,)), dma((3, SLOTS)), dma, dma((rep_n,)),
                dma, dma, dma, dma,
            ],
            compiler_params=pltpu.CompilerParams(
                collective_id=0, has_side_effects=True, vmem_limit_bytes=56 * 2**20
            ),
        )(coords, scale[None, :], nugget[None, :], right_side, site_order[None, :])
        out = jax.ShapeDtypeStruct((months, group_width), F32)
        return pl.pallas_call(
            combine,
            out_shape=(out, out),
            in_specs=[anywhere, vmem],
            out_specs=(anywhere, anywhere),
            scratch_shapes=[
                pltpu.VMEM((4, months, group_width), F32), pltpu.VMEM((2, months, group_width), F32),
                dma((rep_n,)), dma((2, rep_n)),
            ],
            compiler_params=pltpu.CompilerParams(vmem_limit_bytes=56 * 2**20),
        )(powers, factors)

    in_specs = (
        P(None, "sites"),
        P("sites"),
        P("sites"),
        P(None, "sites"),
        P("sites"),
        P(None, ("sites", "rep")),
        P(("sites", "rep")),
    )
    out_specs = (P(None, "sites"), P(None, "sites"))
    return jax.shard_map(local, mesh=mesh, in_specs=in_specs, out_specs=out_specs, check_vma=False)
```

```python
import functools

import jax
import jax.numpy as jnp
from jax import lax
from jax.experimental import pallas as pl
from jax.experimental.pallas import tpu as pltpu
from jax.sharding import PartitionSpec as P

MESH = pl.DeviceIdType.MESH
RANGE_KM = 200.0
TAPER_UNIT = 4.0 / RANGE_KM**5
F32 = jnp.float32
BF16 = jnp.bfloat16
REACH = 4
SLOTS = 2 * REACH + 1
AHEAD = (-2, -3, -1, -4)
BEHIND = (2, 3, 1, 4)
OFFSETS = AHEAD + BEHIND


def split3(value):
    high = value.astype(BF16).astype(F32)
    rest = value - high
    middle = rest.astype(BF16).astype(F32)
    return high, middle, rest - middle


def kernel(
    sizes,
    coords_in, scale_in, nugget_in, right_side_in, order_in,
    out_solution, out_residual,
    coords, scale, nugget, right_side, order,
    data, tile_high, tile_low, geo, halo, last, acc, sums1, sums2, late1, late2, held, made,
    in_sems, out_sem, geo_send, geo_recv, halo_send, halo_recv, last_send, last_recv,
    sum_send, sum_recv, told,
):
    sites_n, rep_n, z_n, y_n = sizes
    months, group_width = right_side.shape
    width = group_width // rep_n
    chain_n = sites_n * rep_n
    my_s = lax.axis_index("sites")
    my_r = lax.axis_index("rep")
    chain = my_s * rep_n + my_r
    my_core = my_s % 2
    my_y = (my_s // 2) % y_n
    my_z = my_s // (2 * y_n)
    n1 = rep_n * y_n
    n2 = 2 * z_n
    place1 = my_r * y_n + my_y
    place2 = my_z * 2 + my_core

    def chain_device(offset):
        other = (chain + offset + chain_n) % chain_n
        return (other // rep_n, other % rep_n)

    def device1(step):
        other = (place1 + step) % n1
        return ((my_z * y_n + other % y_n) * 2 + my_core, other // y_n)

    def device2(step):
        other = (place2 + step) % n2
        return (((other // 2) * y_n + my_y) * 2 + other % 2, my_r)

    barrier = pltpu.get_barrier_semaphore()
    peers = (
        [chain_device(REACH), chain_device(-REACH)]
        + [(my_s, (my_r + step) % rep_n) for step in range(1, rep_n)]
    )
    for peer in peers:
        pl.semaphore_signal(barrier, inc=1, device_id=peer, device_id_type=MESH)

    loads = [
        pltpu.make_async_copy(source, target, in_sems.at[at])
        for at, (source, target) in enumerate((
            (right_side_in, right_side), (coords_in, coords), (scale_in, scale),
            (nugget_in, nugget), (order_in, order),
        ))
    ]
    for load in loads:
        load.start()
    for load in loads:
        load.wait()

    def tell(step):
        for group in (my_s + 2**step, my_s + sites_n - 2**step):
            pl.semaphore_signal(
                told.at[step], inc=1, device_id=(group % sites_n, my_r), device_id_type=MESH
            )

    def hear(step):
        pl.semaphore_wait(told.at[step], 2)

    def await_bytes(ref, sem):
        pltpu.make_async_copy(ref, ref, sem).wait()

    site = jnp.concatenate(
        [coords[...], scale[...], nugget[...], jnp.zeros((4, group_width), F32)], axis=0
    )
    for at, part in enumerate(split3(right_side[...])):
        data[at * months:(at + 1) * months, :] = part.astype(BF16)
    parts = split3(site)
    top = 3 * months
    data[top:top + 16, :] = jnp.concatenate(parts[:2], axis=0).astype(BF16)
    data[top + 16:top + 32, :] = jnp.concatenate(
        [parts[2], jnp.zeros((8, group_width), F32)], axis=0
    ).astype(BF16)
    step_rows = 256
    rows_at = lax.broadcasted_iota(jnp.int32, (step_rows, width), 0)

    def own_group_slot(turn):
        return REACH - my_r + (my_r + turn) % rep_n

    def place_sites(turn, carry):
        slot = own_group_slot(turn)
        start = pl.multiple_of(((my_r + turn) % rep_n) * width, width)
        wanted = order[:, pl.ds(start, width)] - my_s * group_width
        placed = jnp.zeros((top + 32, width), F32)
        for at in range(group_width // step_rows):
            chosen = jnp.where(rows_at == wanted - at * step_rows, 1.0, 0.0).astype(BF16)
            placed = placed + jnp.dot(
                data[:, at * step_rows:(at + 1) * step_rows], chosen, preferred_element_type=F32
            )
        halo[0, slot] = (placed[:months] + placed[months:2 * months]) + placed[2 * months:top]
        geo[slot] = (placed[top:top + 8] + placed[top + 8:top + 16]) + placed[top + 16:top + 24]
        return carry

    lax.fori_loop(0, rep_n, place_sites, 0)
    own_geo = geo[REACH]
    own_scale = own_geo[2:3] * TAPER_UNIT
    own_nugget = own_geo[3:4]

    def split2(vector):
        high = vector.astype(BF16)
        return high, (vector - high.astype(F32)).astype(BF16)

    def parts_of(stage, slot):
        high, low = split2(halo[stage, slot] * geo[slot][2:3])
        return jnp.concatenate([high, low], axis=0), high

    def tile_product(both, high, tiles, rest):
        large = jnp.dot(both, tiles, preferred_element_type=F32)
        small = jnp.dot(high, rest, preferred_element_type=F32)
        return large[:months] + (large[months:] + small)

    def add_product(stage, slot):
        both, high = parts_of(stage, slot)
        acc[...] += tile_product(both, high, tile_high[slot], tile_low[slot])

    def make_tiles(slot, use, out_of_reach=None):
        away = (chain + slot - REACH < 0) | (chain + slot - REACH >= chain_n)
        shift = jnp.where(away, 1.0e6, 0.0).astype(F32)
        columns = jnp.transpose(geo[slot])
        if use:
            both, first = parts_of(0, slot)
        total = jnp.zeros((months, width), F32)
        for at in range(0, width, step_rows):
            lanes = slice(0, width)
            if out_of_reach and out_of_reach[0] == at:
                lanes = slice(0, out_of_reach[1]) if out_of_reach[1] else slice(step_rows, width)
            east = columns[at:at + step_rows, 0:1] + shift
            north = columns[at:at + step_rows, 1:2]
            d_east = east - own_geo[0:1, lanes]
            d_north = north - own_geo[1:2, lanes]
            squared = jnp.clip(d_east * d_east + d_north * d_north, 1.0e-30, RANGE_KM * RANGE_KM)
            distance = squared * lax.rsqrt(squared)
            remain = RANGE_KM - distance
            square = remain * remain
            high, low = split2((square * square) * (distance + 0.25 * RANGE_KM))
            if out_of_reach and out_of_reach[0] == at:
                blank = slice(out_of_reach[1], out_of_reach[1] + step_rows)
                tile_high[slot, at:at + step_rows, blank] = jnp.zeros((step_rows, step_rows), BF16)
                tile_low[slot, at:at + step_rows, blank] = jnp.zeros((step_rows, step_rows), BF16)
            tile_high[slot, at:at + step_rows, lanes] = high
            tile_low[slot, at:at + step_rows, lanes] = low
            if use:
                total = total + tile_product(
                    both[:, at:at + step_rows], first[:, at:at + step_rows], high, low
                )
        if use:
            acc[...] += total

    def image_of(stage):
        return own_scale * acc[...] + own_nugget * halo[stage, REACH]

    pl.semaphore_wait(barrier, len(peers))
    tell(0)

    def upward(turn):
        return turn <= rep_n - 1 - my_r

    def exchange(ref_of, send_sem, recv_of):
        for turn in range(rep_n + 1):
            up = upward(turn)
            source = jnp.where(up, REACH + turn, turn)
            target = jnp.where(up, turn, REACH + turn)
            group = (my_s + jnp.where(up, 1, sites_n - 1)) % sites_n
            pltpu.make_async_remote_copy(
                src_ref=ref_of(source), dst_ref=ref_of(target), send_sem=send_sem, recv_sem=recv_of(target),
                device_id=(group, my_r), device_id_type=MESH,
            ).start()

    exchange(lambda slot: geo.at[slot], geo_send, lambda slot: geo_recv.at[slot])
    exchange(lambda slot: halo.at[0, slot], halo_send.at[0], lambda slot: halo_recv.at[0, slot])

    acc[...] = jnp.zeros_like(acc)

    def own_pieces(turn, carry):
        make_tiles(own_group_slot(turn), True)
        return carry

    lax.fori_loop(0, rep_n, own_pieces, 0)
    hear(0)
    tell(1)

    def come_slot(turn):
        return jnp.where(upward(turn), turn, REACH + turn)

    def other_tiles(turn, carry):
        slot = come_slot(turn)
        await_bytes(geo.at[slot], geo_recv.at[slot])
        make_tiles(slot, False)
        return carry

    await_bytes(geo.at[0], geo_recv.at[0])
    make_tiles(0, False, (0, width - step_rows))
    lax.fori_loop(1, rep_n, other_tiles, 0)
    await_bytes(geo.at[2 * REACH], geo_recv.at[2 * REACH])
    make_tiles(2 * REACH, False, (width - step_rows, 0))
    hear(1)
    tell(2)
    for turn in range(rep_n + 1):
        slot = come_slot(turn)
        await_bytes(halo.at[0, slot], halo_recv.at[0, slot])
        add_product(0, slot)

    def spread_halo(stage):
        for offset in OFFSETS:
            pltpu.make_async_remote_copy(
                src_ref=halo.at[stage, REACH], dst_ref=halo.at[stage, REACH - offset],
                send_sem=halo_send.at[stage], recv_sem=halo_recv.at[stage, REACH - offset],
                device_id=chain_device(offset), device_id_type=MESH,
            ).start()

    def add_side(stage, offsets):
        for offset in offsets:
            slot = REACH - offset
            await_bytes(halo.at[stage, slot], halo_recv.at[stage, slot])
            add_product(stage, slot)

    def folded(first, second):
        value = first * second
        total = value[:, :128]
        for at in range(128, width, 128):
            total = total + value[:, at:at + 128]
        return total

    def as_row(pieces):
        return jnp.sum(jnp.transpose(jnp.concatenate(pieces, axis=0)), axis=0, keepdims=True)

    def columns_of(row):
        return jnp.transpose(jnp.concatenate([row, jnp.zeros((8 - row.shape[0], 128), F32)], axis=0))

    def begin_sum(slots, send_sem, recv_sem):
        for step in range(1, n1):
            pltpu.make_async_remote_copy(
                src_ref=slots.at[place1], dst_ref=slots.at[place1], send_sem=send_sem, recv_sem=recv_sem,
                device_id=device1(step), device_id_type=MESH,
            ).start()

    def pass_sum(slots, recv_sem, slots_next, send_sem_next, recv_sem_next):
        await_bytes(slots.at[pl.ds(0, n1 - 1)], recv_sem)
        slots_next[place2] = jnp.sum(slots[...], axis=0)
        for step in range(1, n2):
            pltpu.make_async_remote_copy(
                src_ref=slots_next.at[place2], dst_ref=slots_next.at[place2],
                send_sem=send_sem_next, recv_sem=recv_sem_next,
                device_id=device2(step), device_id_type=MESH,
            ).start()

    def end_sum(slots, recv_sem):
        await_bytes(slots.at[pl.ds(0, n2 - 1)], recv_sem)
        return columns_of(jnp.sum(slots[...], axis=0))

    halo[1, REACH] = image_of(0)
    spread_halo(1)
    acc[...] = jnp.zeros_like(acc)
    add_product(1, REACH)
    hear(2)
    tell(3)
    add_side(1, AHEAD)
    hear(3)
    tell(4)
    add_side(1, BEHIND)
    halo[2, REACH] = image_of(1)
    spread_halo(2)
    start, first, second = halo[0, REACH], halo[1, REACH], halo[2, REACH]
    sums1[place1, 0:1] = as_row(
        [folded(start, start), folded(start, first), folded(first, first), folded(first, second)]
    )
    sums1[place1, 1:2] = as_row([folded(second, second), jnp.zeros((128 - months, 128), F32)])
    begin_sum(sums1, sum_send.at[0], sum_recv.at[0])
    acc[...] = jnp.zeros_like(acc)
    add_product(2, REACH)
    within = acc[...]
    add_side(2, AHEAD)
    doubled = own_scale * (2.0 * acc[...] - within) + own_nugget * halo[2, REACH]
    late1[place1] = as_row([folded(halo[2, REACH], doubled), jnp.zeros((128 - months, 128), F32)])
    begin_sum(late1, sum_send.at[2], sum_recv.at[2])
    hear(4)
    pass_sum(sums1, sum_recv.at[0], sums2, sum_send.at[1], sum_recv.at[1])
    add_side(2, BEHIND)
    last[my_r] = image_of(2)
    for step in range(1, rep_n):
        pltpu.make_async_remote_copy(
            src_ref=last.at[my_r], dst_ref=last.at[my_r],
            send_sem=last_send, recv_sem=last_recv.at[step],
            device_id=(my_s, (my_r + step) % rep_n), device_id_type=MESH,
        ).start()
    pass_sum(late1, sum_recv.at[2], late2, sum_send.at[3], sum_recv.at[3])

    total = end_sum(sums2, sum_recv.at[1])
    m0, m1, m2, m3 = [total[at * months:(at + 1) * months, 0:1] for at in range(4)]
    m4 = total[:months, 1:2]
    alpha0 = m0 / m1
    norm1 = alpha0 * alpha0 * m2 - m0
    lead = 1.0 + norm1 / m0
    alpha1 = norm1 / (alpha0 * (alpha0 * m3 - lead * m2))
    r1 = -(alpha0 + alpha1 * lead)
    r2 = alpha0 * alpha1
    norm2 = r2 * (m2 + r1 * m3 + r2 * m4)
    beta2 = norm2 / norm1
    d0 = 1.0 + beta2 * lead
    d1 = r1 - beta2 * alpha0
    for step in range(1, rep_n):
        await_bytes(last.at[0], last_recv.at[step])
    for place in range(rep_n):
        lanes = slice(place * width, (place + 1) * width)
        slot = REACH + place - my_r
        start, first, second = halo[0, slot], halo[1, slot], halo[2, slot]
        held[0, :, lanes] = (alpha0 + alpha1 * lead) * start - (alpha1 * alpha0) * first
        held[1, :, lanes] = d0 * start + d1 * first + r2 * second
        held[2, :, lanes] = start + r1 * first + r2 * second
        held[3, :, lanes] = d0 * first + d1 * second + r2 * last[place]
    count = len(OFFSETS)
    await_bytes(geo.at[pl.ds(0, rep_n + 1)], geo_send)
    await_bytes(halo.at[0, pl.ds(0, rep_n + 1)], halo_send.at[0])
    for stage in range(1, 3):
        await_bytes(halo.at[stage, pl.ds(0, count)], halo_send.at[stage])
    await_bytes(last.at[pl.ds(0, rep_n - 1)], last_send)
    await_bytes(sums1.at[pl.ds(0, n1 - 1)], sum_send.at[0])
    await_bytes(sums2.at[pl.ds(0, n2 - 1)], sum_send.at[1])
    await_bytes(late1.at[pl.ds(0, n1 - 1)], sum_send.at[2])

    m5 = end_sum(late2, sum_recv.at[3])[:months, 0:1]
    alpha2 = norm2 / (r2 * (d0 * m3 + d1 * m4 + r2 * m5))
    stores = []
    for place in range(rep_n):
        lanes = slice(place * width, (place + 1) * width)
        made[0, :, lanes] = held[0, :, lanes] + alpha2 * held[1, :, lanes]
        made[1, :, lanes] = held[2, :, lanes] - alpha2 * held[3, :, lanes]
        for which, out in enumerate((out_solution, out_residual)):
            store = pltpu.make_async_copy(made.at[which, :, lanes], out.at[:, lanes], out_sem.at[which, place])
            store.start()
            stores.append(store)
    for store in stores:
        store.wait()
    await_bytes(late2.at[pl.ds(0, n2 - 1)], sum_send.at[3])


def solution(mesh):
    sites_n, rep_n = mesh.shape["sites"], mesh.shape["rep"]
    y_n = 4
    z_n = sites_n // (2 * y_n)

    def local(coords, scale, nugget, right_side, site_order, pair_list, pair_count):
        months, group_width = right_side.shape
        width = group_width // rep_n
        anywhere = pl.BlockSpec(memory_space=pl.ANY)
        dma = pltpu.SemaphoreType.DMA
        out = jax.ShapeDtypeStruct((months, group_width), F32)
        return pl.pallas_call(
            functools.partial(kernel, (sites_n, rep_n, z_n, y_n)),
            out_shape=(out, out),
            in_specs=[anywhere] * 5,
            out_specs=(anywhere, anywhere),
            scratch_shapes=[
                pltpu.VMEM((2, group_width), F32),
                pltpu.VMEM((1, group_width), F32),
                pltpu.VMEM((1, group_width), F32),
                pltpu.VMEM((months, group_width), F32),
                pltpu.VMEM((1, group_width), jnp.int32),
                pltpu.VMEM((3 * months + 32, group_width), BF16),
                pltpu.VMEM((SLOTS, width, width), BF16),
                pltpu.VMEM((SLOTS, width, width), BF16),
                pltpu.VMEM((SLOTS, 8, width), F32),
                pltpu.VMEM((3, SLOTS, months, width), F32),
                pltpu.VMEM((rep_n, months, width), F32),
                pltpu.VMEM((months, width), F32),
                pltpu.VMEM((rep_n * y_n, 2, 128), F32),
                pltpu.VMEM((2 * z_n, 2, 128), F32),
                pltpu.VMEM((rep_n * y_n, 1, 128), F32),
                pltpu.VMEM((2 * z_n, 1, 128), F32),
                pltpu.VMEM((4, months, group_width), F32),
                pltpu.VMEM((2, months, group_width), F32),
                dma((5,)), dma((2, rep_n)), dma, dma((SLOTS,)), dma((3,)), dma((3, SLOTS)), dma, dma((rep_n,)),
                dma((4,)), dma((4,)), pltpu.SemaphoreType.REGULAR((5,)),
            ],
            compiler_params=pltpu.CompilerParams(
                collective_id=0, has_side_effects=True, vmem_limit_bytes=56 * 2**20
            ),
        )(coords, scale[None, :], nugget[None, :], right_side, site_order[None, :])

    in_specs = (
        P(None, "sites"),
        P("sites"),
        P("sites"),
        P(None, "sites"),
        P("sites"),
        P(None, ("sites", "rep")),
        P(("sites", "rep")),
    )
    out_specs = (P(None, "sites"), P(None, "sites"))
    return jax.shard_map(local, mesh=mesh, in_specs=in_specs, out_specs=out_specs, check_vma=False)
```

```python
import functools

import jax
import jax.numpy as jnp
from jax import lax
from jax.experimental import pallas as pl
from jax.experimental.pallas import tpu as pltpu
from jax.sharding import PartitionSpec as P

MESH = pl.DeviceIdType.MESH
RANGE_KM = 200.0
TAPER_UNIT = 4.0 / RANGE_KM**5
F32 = jnp.float32
BF16 = jnp.bfloat16
REACH = 4
SLOTS = 2 * REACH + 1
AHEAD = (-2, -3, -1, -4)
BEHIND = (2, 3, 1, 4)
OFFSETS = AHEAD + BEHIND


def split3(value):
    high = value.astype(BF16).astype(F32)
    rest = value - high
    middle = rest.astype(BF16).astype(F32)
    return high, middle, rest - middle


def swing(count):
    return sorted(range(count), key=lambda ahead: -min(ahead, count - ahead))


def kernel(
    sizes,
    coords_in, scale_in, nugget_in, right_side_in, order_in,
    out_solution, out_residual,
    coords, scale, nugget, right_side, order,
    data, tile_high, tile_low, geo, halo, last, acc, sums1, sums2, late, pair, made,
    in_sems, out_sem, geo_send, geo_recv, halo_send, halo_recv, last_send, last_recv,
    sum_send, sum_recv, pair_sems, told,
):
    sites_n, rep_n, z_n, y_n = sizes
    months, group_width = right_side.shape
    width = group_width // rep_n
    chain_n = sites_n * rep_n
    my_s = lax.axis_index("sites")
    my_r = lax.axis_index("rep")
    chain = my_s * rep_n + my_r
    my_core = my_s % 2
    my_y = (my_s // 2) % y_n
    my_z = my_s // (2 * y_n)
    n1 = rep_n * y_n
    n2 = 2 * z_n
    place1 = my_r * y_n + my_y
    place2 = my_z * 2 + my_core
    chip = (my_s // 2) * rep_n + my_r

    def chain_device(offset):
        other = (chain + offset + chain_n) % chain_n
        return (other // rep_n, other % rep_n)

    def device1(step):
        other = (place1 + step) % n1
        return ((my_z * y_n + other % y_n) * 2 + my_core, other // y_n)

    def device2(step):
        other = (place2 + step) % n2
        return (((other // 2) * y_n + my_y) * 2 + other % 2, my_r)

    barrier = pltpu.get_barrier_semaphore()
    peers = (
        [chain_device(REACH), chain_device(-REACH)]
        + [(my_s, (my_r + step) % rep_n) for step in range(1, rep_n)]
    )
    for peer in peers:
        pl.semaphore_signal(barrier, inc=1, device_id=peer, device_id_type=MESH)

    loads = [
        pltpu.make_async_copy(source, target, in_sems.at[at])
        for at, (source, target) in enumerate((
            (right_side_in, right_side), (coords_in, coords), (scale_in, scale),
            (nugget_in, nugget), (order_in, order),
        ))
    ]
    for load in loads:
        load.start()
    for load in loads:
        load.wait()

    def tell(step):
        for group in (my_s + 2**step, my_s + sites_n - 2**step):
            pl.semaphore_signal(
                told.at[step], inc=1, device_id=(group % sites_n, my_r), device_id_type=MESH
            )

    def hear(step):
        pl.semaphore_wait(told.at[step], 2)

    def await_bytes(ref, sem):
        pltpu.make_async_copy(ref, ref, sem).wait()

    site = jnp.concatenate(
        [coords[...], scale[...], nugget[...], jnp.zeros((4, group_width), F32)], axis=0
    )
    for at, part in enumerate(split3(right_side[...])):
        data[at * months:(at + 1) * months, :] = part.astype(BF16)
    parts = split3(site)
    top = 3 * months
    data[top:top + 16, :] = jnp.concatenate(parts[:2], axis=0).astype(BF16)
    data[top + 16:top + 32, :] = jnp.concatenate(
        [parts[2], jnp.zeros((8, group_width), F32)], axis=0
    ).astype(BF16)
    step_rows = 256
    rows_at = lax.broadcasted_iota(jnp.int32, (step_rows, width), 0)

    def own_group_slot(turn):
        return REACH - my_r + (my_r + turn) % rep_n

    def place_sites(turn, carry):
        slot = own_group_slot(turn)
        start = pl.multiple_of(((my_r + turn) % rep_n) * width, width)
        wanted = order[:, pl.ds(start, width)] - my_s * group_width
        placed = jnp.zeros((top + 32, width), F32)
        for at in range(group_width // step_rows):
            chosen = jnp.where(rows_at == wanted - at * step_rows, 1.0, 0.0).astype(BF16)
            placed = placed + jnp.dot(
                data[:, at * step_rows:(at + 1) * step_rows], chosen, preferred_element_type=F32
            )
        halo[0, slot] = (placed[:months] + placed[months:2 * months]) + placed[2 * months:top]
        geo[slot] = (placed[top:top + 8] + placed[top + 8:top + 16]) + placed[top + 16:top + 24]
        return carry

    lax.fori_loop(0, rep_n, place_sites, 0)
    own_geo = geo[REACH]
    own_scale = own_geo[2:3] * TAPER_UNIT
    own_nugget = own_geo[3:4]

    def split2(vector):
        high = vector.astype(BF16)
        return high, (vector - high.astype(F32)).astype(BF16)

    def parts_of(stage, slot):
        high, low = split2(halo[stage, slot] * geo[slot][2:3])
        return jnp.concatenate([high, low], axis=0), high

    def tile_product(both, high, tiles, rest):
        large = jnp.dot(both, tiles, preferred_element_type=F32)
        small = jnp.dot(high, rest, preferred_element_type=F32)
        return large[:months] + (large[months:] + small)

    def add_product(stage, slot):
        both, high = parts_of(stage, slot)
        acc[...] += tile_product(both, high, tile_high[slot], tile_low[slot])

    def make_tiles(slot, use, out_of_reach=None):
        away = (chain + slot - REACH < 0) | (chain + slot - REACH >= chain_n)
        shift = jnp.where(away, 1.0e6, 0.0).astype(F32)
        columns = jnp.transpose(geo[slot])
        if use:
            both, first = parts_of(0, slot)
        total = jnp.zeros((months, width), F32)
        for at in range(0, width, step_rows):
            lanes = slice(0, width)
            if out_of_reach and out_of_reach[0] == at:
                lanes = slice(0, out_of_reach[1]) if out_of_reach[1] else slice(step_rows, width)
            east = columns[at:at + step_rows, 0:1] + shift
            north = columns[at:at + step_rows, 1:2]
            d_east = east - own_geo[0:1, lanes]
            d_north = north - own_geo[1:2, lanes]
            squared = jnp.clip(d_east * d_east + d_north * d_north, 1.0e-30, RANGE_KM * RANGE_KM)
            distance = squared * lax.rsqrt(squared)
            remain = RANGE_KM - distance
            square = remain * remain
            high, low = split2((square * square) * (distance + 0.25 * RANGE_KM))
            if out_of_reach and out_of_reach[0] == at:
                blank = slice(out_of_reach[1], out_of_reach[1] + step_rows)
                tile_high[slot, at:at + step_rows, blank] = jnp.zeros((step_rows, step_rows), BF16)
                tile_low[slot, at:at + step_rows, blank] = jnp.zeros((step_rows, step_rows), BF16)
            tile_high[slot, at:at + step_rows, lanes] = high
            tile_low[slot, at:at + step_rows, lanes] = low
            if use:
                total = total + tile_product(
                    both[:, at:at + step_rows], first[:, at:at + step_rows], high, low
                )
        if use:
            acc[...] += total

    def image_of(stage):
        return own_scale * acc[...] + own_nugget * halo[stage, REACH]

    pl.semaphore_wait(barrier, len(peers))
    tell(0)

    def upward(turn):
        return turn <= rep_n - 1 - my_r

    def exchange(ref_of, send_sem, recv_of):
        for turn in range(rep_n + 1):
            up = upward(turn)
            source = jnp.where(up, REACH + turn, turn)
            target = jnp.where(up, turn, REACH + turn)
            group = (my_s + jnp.where(up, 1, sites_n - 1)) % sites_n
            pltpu.make_async_remote_copy(
                src_ref=ref_of(source), dst_ref=ref_of(target), send_sem=send_sem, recv_sem=recv_of(target),
                device_id=(group, my_r), device_id_type=MESH,
            ).start()

    exchange(lambda slot: geo.at[slot], geo_send, lambda slot: geo_recv.at[slot])
    exchange(lambda slot: halo.at[0, slot], halo_send.at[0], lambda slot: halo_recv.at[0, slot])

    acc[...] = jnp.zeros_like(acc)

    def own_pieces(turn, carry):
        make_tiles(own_group_slot(turn), True)
        return carry

    lax.fori_loop(0, rep_n, own_pieces, 0)
    hear(0)
    tell(1)

    def come_slot(turn):
        return jnp.where(upward(turn), turn, REACH + turn)

    def other_tiles(turn, carry):
        slot = come_slot(turn)
        await_bytes(geo.at[slot], geo_recv.at[slot])
        make_tiles(slot, False)
        return carry

    await_bytes(geo.at[0], geo_recv.at[0])
    make_tiles(0, False, (0, width - step_rows))
    lax.fori_loop(1, rep_n, other_tiles, 0)
    await_bytes(geo.at[2 * REACH], geo_recv.at[2 * REACH])
    make_tiles(2 * REACH, False, (width - step_rows, 0))
    hear(1)
    tell(2)
    for turn in range(rep_n + 1):
        slot = come_slot(turn)
        await_bytes(halo.at[0, slot], halo_recv.at[0, slot])
        add_product(0, slot)

    def spread_halo(stage):
        for offset in OFFSETS:
            pltpu.make_async_remote_copy(
                src_ref=halo.at[stage, REACH], dst_ref=halo.at[stage, REACH - offset],
                send_sem=halo_send.at[stage], recv_sem=halo_recv.at[stage, REACH - offset],
                device_id=chain_device(offset), device_id_type=MESH,
            ).start()

    def add_side(stage, offsets):
        for offset in offsets:
            slot = REACH - offset
            await_bytes(halo.at[stage, slot], halo_recv.at[stage, slot])
            add_product(stage, slot)

    def folded(first, second):
        value = first * second
        total = value[:, :128]
        for at in range(128, width, 128):
            total = total + value[:, at:at + 128]
        return total

    def as_row(pieces):
        return jnp.sum(jnp.transpose(jnp.concatenate(pieces, axis=0)), axis=0, keepdims=True)

    def columns_of(row):
        return jnp.transpose(jnp.concatenate([row, jnp.zeros((8 - row.shape[0], 128), F32)], axis=0))

    def begin_sum(slots, send_sem, recv_sem):
        for step in range(1, n1):
            pltpu.make_async_remote_copy(
                src_ref=slots.at[place1], dst_ref=slots.at[place1], send_sem=send_sem, recv_sem=recv_sem,
                device_id=device1(step), device_id_type=MESH,
            ).start()

    def pass_sum(slots, recv_sem, slots_next, send_sem_next, recv_sem_next):
        await_bytes(slots.at[pl.ds(0, n1 - 1)], recv_sem)
        slots_next[place2] = jnp.sum(slots[...], axis=0)
        for step in range(1, n2):
            pltpu.make_async_remote_copy(
                src_ref=slots_next.at[place2], dst_ref=slots_next.at[place2],
                send_sem=send_sem_next, recv_sem=recv_sem_next,
                device_id=device2(step), device_id_type=MESH,
            ).start()

    def end_sum(slots, recv_sem):
        await_bytes(slots.at[pl.ds(0, n2 - 1)], recv_sem)
        return columns_of(jnp.sum(slots[...], axis=0))

    halo[1, REACH] = image_of(0)
    spread_halo(1)
    acc[...] = jnp.zeros_like(acc)
    add_product(1, REACH)
    start, first = halo[0, REACH], halo[1, REACH]
    sums1[place1] = as_row([
        folded(start, start), folded(start, first), folded(first, first), jnp.zeros((128 - 3 * months, 128), F32)
    ])
    hear(2)
    tell(3)
    begin_sum(sums1, sum_send.at[0], sum_recv.at[0])
    add_side(1, AHEAD)
    hear(3)
    tell(4)
    add_side(1, BEHIND)
    halo[2, REACH] = image_of(1)
    spread_halo(2)
    hear(4)
    pass_sum(sums1, sum_recv.at[0], sums2, sum_send.at[1], sum_recv.at[1])
    second = halo[2, REACH]
    known = [folded(halo[1, REACH], second), folded(second, second)]
    acc[...] = jnp.zeros_like(acc)
    add_product(2, REACH)
    within = acc[...]
    add_side(2, AHEAD)
    doubled = own_scale * (2.0 * acc[...] - within) + own_nugget * halo[2, REACH]
    pair[my_core] = as_row(
        known + [folded(halo[2, REACH], doubled), jnp.zeros((128 - 3 * months, 128), F32)]
    )
    pair_copy = pltpu.make_async_remote_copy(
        src_ref=pair.at[my_core], dst_ref=pair.at[my_core], send_sem=pair_sems.at[0], recv_sem=pair_sems.at[1],
        device_id=(my_s + 1 - 2 * my_core, my_r), device_id_type=MESH,
    )
    pair_copy.start()
    await_bytes(pair.at[0], pair_sems.at[1])
    late[chip] = pair[0] + pair[1]
    for ahead_z in swing(z_n):
        for ahead_y in swing(y_n):
            row = ((my_z + ahead_z) % z_n) * y_n + (my_y + ahead_y) % y_n
            for ahead_r in swing(rep_n):
                if ahead_z or ahead_y or ahead_r:
                    pltpu.make_async_remote_copy(
                        src_ref=late.at[chip], dst_ref=late.at[chip],
                        send_sem=sum_send.at[2], recv_sem=sum_recv.at[2],
                        device_id=(row * 2 + my_core, (my_r + ahead_r) % rep_n), device_id_type=MESH,
                    ).start()
    add_side(2, BEHIND)
    last[my_r] = image_of(2)
    for step in range(1, rep_n):
        pltpu.make_async_remote_copy(
            src_ref=last.at[my_r], dst_ref=last.at[my_r],
            send_sem=last_send, recv_sem=last_recv.at[step],
            device_id=(my_s, (my_r + step) % rep_n), device_id_type=MESH,
        ).start()

    def thirds(columns):
        return [columns[at * months:(at + 1) * months, 0:1] for at in range(3)]

    m0, m1, m2 = thirds(end_sum(sums2, sum_recv.at[1]))
    alpha0 = m0 / m1
    norm1 = alpha0 * alpha0 * m2 - m0
    lead = 1.0 + norm1 / m0
    for step in range(1, rep_n):
        await_bytes(last.at[0], last_recv.at[step])
    count = len(OFFSETS)
    await_bytes(geo.at[pl.ds(0, rep_n + 1)], geo_send)
    await_bytes(halo.at[0, pl.ds(0, rep_n + 1)], halo_send.at[0])
    for stage in range(1, 3):
        await_bytes(halo.at[stage, pl.ds(0, count)], halo_send.at[stage])
    await_bytes(last.at[pl.ds(0, rep_n - 1)], last_send)
    await_bytes(sums1.at[pl.ds(0, n1 - 1)], sum_send.at[0])
    await_bytes(sums2.at[pl.ds(0, n2 - 1)], sum_send.at[1])

    await_bytes(late.at[pl.ds(0, chain_n // 2 - 1)], sum_recv.at[2])
    m3, m4, m5 = thirds(columns_of(jnp.sum(late[...], axis=0)))
    alpha1 = norm1 / (alpha0 * (alpha0 * m3 - lead * m2))
    r1 = -(alpha0 + alpha1 * lead)
    r2 = alpha0 * alpha1
    norm2 = r2 * (m2 + r1 * m3 + r2 * m4)
    beta2 = norm2 / norm1
    d0 = 1.0 + beta2 * lead
    d1 = r1 - beta2 * alpha0
    alpha2 = norm2 / (r2 * (d0 * m3 + d1 * m4 + r2 * m5))
    found = (alpha2 * d0 - r1, alpha2 * d1 - r2, alpha2 * r2)
    left = (r1 - alpha2 * d0, r2 - alpha2 * d1, -alpha2 * r2)
    stores = []
    for place in range(rep_n):
        lanes = slice(place * width, (place + 1) * width)
        slot = REACH + place - my_r
        start, first, second = halo[0, slot], halo[1, slot], halo[2, slot]
        made[0, :, lanes] = found[0] * start + found[1] * first + found[2] * second
        made[1, :, lanes] = start + left[0] * first + left[1] * second + left[2] * last[place]
        for which, out in enumerate((out_solution, out_residual)):
            store = pltpu.make_async_copy(made.at[which, :, lanes], out.at[:, lanes], out_sem.at[which, place])
            store.start()
            stores.append(store)
    for store in stores:
        store.wait()
    await_bytes(late.at[pl.ds(0, chain_n // 2 - 1)], sum_send.at[2])
    await_bytes(pair.at[0], pair_sems.at[0])


def solution(mesh):
    sites_n, rep_n = mesh.shape["sites"], mesh.shape["rep"]
    y_n = 4
    z_n = sites_n // (2 * y_n)

    def local(coords, scale, nugget, right_side, site_order, pair_list, pair_count):
        months, group_width = right_side.shape
        width = group_width // rep_n
        anywhere = pl.BlockSpec(memory_space=pl.ANY)
        dma = pltpu.SemaphoreType.DMA
        out = jax.ShapeDtypeStruct((months, group_width), F32)
        return pl.pallas_call(
            functools.partial(kernel, (sites_n, rep_n, z_n, y_n)),
            out_shape=(out, out),
            in_specs=[anywhere] * 5,
            out_specs=(anywhere, anywhere),
            scratch_shapes=[
                pltpu.VMEM((2, group_width), F32),
                pltpu.VMEM((1, group_width), F32),
                pltpu.VMEM((1, group_width), F32),
                pltpu.VMEM((months, group_width), F32),
                pltpu.VMEM((1, group_width), jnp.int32),
                pltpu.VMEM((3 * months + 32, group_width), BF16),
                pltpu.VMEM((SLOTS, width, width), BF16),
                pltpu.VMEM((SLOTS, width, width), BF16),
                pltpu.VMEM((SLOTS, 8, width), F32),
                pltpu.VMEM((3, SLOTS, months, width), F32),
                pltpu.VMEM((rep_n, months, width), F32),
                pltpu.VMEM((months, width), F32),
                pltpu.VMEM((rep_n * y_n, 1, 128), F32),
                pltpu.VMEM((2 * z_n, 1, 128), F32),
                pltpu.VMEM((sites_n * rep_n // 2, 1, 128), F32),
                pltpu.VMEM((2, 1, 128), F32),
                pltpu.VMEM((2, months, group_width), F32),
                dma((5,)), dma((2, rep_n)), dma, dma((SLOTS,)), dma((3,)), dma((3, SLOTS)), dma, dma((rep_n,)),
                dma((3,)), dma((3,)), dma((2,)), pltpu.SemaphoreType.REGULAR((5,)),
            ],
            compiler_params=pltpu.CompilerParams(
                collective_id=0, has_side_effects=True, vmem_limit_bytes=56 * 2**20
            ),
        )(coords, scale[None, :], nugget[None, :], right_side, site_order[None, :])

    in_specs = (
        P(None, "sites"),
        P("sites"),
        P("sites"),
        P(None, "sites"),
        P("sites"),
        P(None, ("sites", "rep")),
        P(("sites", "rep")),
    )
    out_specs = (P(None, "sites"), P(None, "sites"))
    return jax.shard_map(local, mesh=mesh, in_specs=in_specs, out_specs=out_specs, check_vma=False)
```

```python
import functools

import jax
import jax.numpy as jnp
from jax import lax
from jax.experimental import pallas as pl
from jax.experimental.pallas import tpu as pltpu
from jax.sharding import PartitionSpec as P

MESH = pl.DeviceIdType.MESH
RANGE_KM = 200.0
TAPER_UNIT = 4.0 / RANGE_KM**5
F32 = jnp.float32
BF16 = jnp.bfloat16
REACH = 4
SLOTS = 2 * REACH + 1
AHEAD = (-2, -3, -1, -4)
BEHIND = (2, 3, 1, 4)
OFFSETS = AHEAD + BEHIND


def split3(value):
    high = value.astype(BF16).astype(F32)
    rest = value - high
    middle = rest.astype(BF16).astype(F32)
    return high, middle, rest - middle


def swing(count):
    return sorted(range(count), key=lambda ahead: -min(ahead, count - ahead))


def kernel(
    sizes,
    coords_in, scale_in, nugget_in, right_side_in, order_in,
    out_solution, out_residual,
    coords, scale, nugget, right_side, order,
    data, tile_high, tile_low, geo, halo, last, acc, sums1, sums2, late, pair,
    in_sems, geo_send, geo_recv, halo_send, halo_recv, last_send, last_recv,
    sum_send, sum_recv, pair_sems, told,
):
    sites_n, rep_n, z_n, y_n = sizes
    months, group_width = right_side.shape
    width = group_width // rep_n
    chain_n = sites_n * rep_n
    my_s = lax.axis_index("sites")
    my_r = lax.axis_index("rep")
    chain = my_s * rep_n + my_r
    my_core = my_s % 2
    my_y = (my_s // 2) % y_n
    my_z = my_s // (2 * y_n)
    n1 = rep_n * y_n
    n2 = 2 * z_n
    place1 = my_r * y_n + my_y
    place2 = my_z * 2 + my_core
    chip = (my_s // 2) * rep_n + my_r

    def chain_device(offset):
        other = (chain + offset + chain_n) % chain_n
        return (other // rep_n, other % rep_n)

    def device1(step):
        other = (place1 + step) % n1
        return ((my_z * y_n + other % y_n) * 2 + my_core, other // y_n)

    def device2(step):
        other = (place2 + step) % n2
        return (((other // 2) * y_n + my_y) * 2 + other % 2, my_r)

    barrier = pltpu.get_barrier_semaphore()
    peers = (
        [chain_device(REACH), chain_device(-REACH)]
        + [(my_s, (my_r + step) % rep_n) for step in range(1, rep_n)]
    )
    for peer in peers:
        pl.semaphore_signal(barrier, inc=1, device_id=peer, device_id_type=MESH)

    loads = [
        pltpu.make_async_copy(source, target, in_sems.at[at])
        for at, (source, target) in enumerate((
            (right_side_in, right_side), (coords_in, coords), (scale_in, scale),
            (nugget_in, nugget), (order_in, order),
        ))
    ]
    for load in loads:
        load.start()
    for load in loads:
        load.wait()

    def tell(step):
        for group in (my_s + 2**step, my_s + sites_n - 2**step):
            pl.semaphore_signal(
                told.at[step], inc=1, device_id=(group % sites_n, my_r), device_id_type=MESH
            )

    def hear(step):
        pl.semaphore_wait(told.at[step], 2)

    def await_bytes(ref, sem):
        pltpu.make_async_copy(ref, ref, sem).wait()

    site = jnp.concatenate(
        [coords[...], scale[...], nugget[...], jnp.zeros((4, group_width), F32)], axis=0
    )
    for at, part in enumerate(split3(right_side[...])):
        data[at * months:(at + 1) * months, :] = part.astype(BF16)
    parts = split3(site)
    top = 3 * months
    data[top:top + 16, :] = jnp.concatenate(parts[:2], axis=0).astype(BF16)
    data[top + 16:top + 32, :] = jnp.concatenate(
        [parts[2], jnp.zeros((8, group_width), F32)], axis=0
    ).astype(BF16)
    step_rows = 256
    rows_at = lax.broadcasted_iota(jnp.int32, (step_rows, width), 0)

    def own_group_slot(turn):
        return REACH - my_r + (my_r + turn) % rep_n

    def place_sites(turn, carry):
        slot = own_group_slot(turn)
        start = pl.multiple_of(((my_r + turn) % rep_n) * width, width)
        wanted = order[:, pl.ds(start, width)] - my_s * group_width
        placed = jnp.zeros((top + 32, width), F32)
        for at in range(group_width // step_rows):
            chosen = jnp.where(rows_at == wanted - at * step_rows, 1.0, 0.0).astype(BF16)
            placed = placed + jnp.dot(
                data[:, at * step_rows:(at + 1) * step_rows], chosen, preferred_element_type=F32
            )
        halo[0, slot] = (placed[:months] + placed[months:2 * months]) + placed[2 * months:top]
        geo[slot] = (placed[top:top + 8] + placed[top + 8:top + 16]) + placed[top + 16:top + 24]
        return carry

    lax.fori_loop(0, rep_n, place_sites, 0)
    own_geo = geo[REACH]
    own_scale = own_geo[2:3] * TAPER_UNIT
    own_nugget = own_geo[3:4]

    def split2(vector):
        high = vector.astype(BF16)
        return high, (vector - high.astype(F32)).astype(BF16)

    def parts_of(stage, slot):
        high, low = split2(halo[stage, slot] * geo[slot][2:3])
        return jnp.concatenate([high, low], axis=0), high

    def tile_product(both, high, tiles, rest):
        large = jnp.dot(both, tiles, preferred_element_type=F32)
        small = jnp.dot(high, rest, preferred_element_type=F32)
        return large[:months] + (large[months:] + small)

    def add_product(stage, slot):
        both, high = parts_of(stage, slot)
        acc[...] += tile_product(both, high, tile_high[slot], tile_low[slot])

    def make_tiles(slot, use, out_of_reach=None):
        away = (chain + slot - REACH < 0) | (chain + slot - REACH >= chain_n)
        shift = jnp.where(away, 1.0e6, 0.0).astype(F32)
        columns = jnp.transpose(geo[slot])
        if use:
            both, first = parts_of(0, slot)
        total = jnp.zeros((months, width), F32)
        for at in range(0, width, step_rows):
            lanes = slice(0, width)
            if out_of_reach and out_of_reach[0] == at:
                lanes = slice(0, out_of_reach[1]) if out_of_reach[1] else slice(step_rows, width)
            east = columns[at:at + step_rows, 0:1] + shift
            north = columns[at:at + step_rows, 1:2]
            d_east = east - own_geo[0:1, lanes]
            d_north = north - own_geo[1:2, lanes]
            squared = jnp.clip(d_east * d_east + d_north * d_north, 1.0e-30, RANGE_KM * RANGE_KM)
            distance = squared * lax.rsqrt(squared)
            remain = RANGE_KM - distance
            square = remain * remain
            high, low = split2((square * square) * (distance + 0.25 * RANGE_KM))
            if out_of_reach and out_of_reach[0] == at:
                blank = slice(out_of_reach[1], out_of_reach[1] + step_rows)
                tile_high[slot, at:at + step_rows, blank] = jnp.zeros((step_rows, step_rows), BF16)
                tile_low[slot, at:at + step_rows, blank] = jnp.zeros((step_rows, step_rows), BF16)
            tile_high[slot, at:at + step_rows, lanes] = high
            tile_low[slot, at:at + step_rows, lanes] = low
            if use:
                total = total + tile_product(
                    both[:, at:at + step_rows], first[:, at:at + step_rows], high, low
                )
        if use:
            acc[...] += total

    def image_of(stage):
        return own_scale * acc[...] + own_nugget * halo[stage, REACH]

    pl.semaphore_wait(barrier, len(peers))
    tell(0)

    def upward(turn):
        return turn <= rep_n - 1 - my_r

    def exchange(ref_of, send_sem, recv_of):
        for turn in range(rep_n + 1):
            up = upward(turn)
            source = jnp.where(up, REACH + turn, turn)
            target = jnp.where(up, turn, REACH + turn)
            group = (my_s + jnp.where(up, 1, sites_n - 1)) % sites_n
            pltpu.make_async_remote_copy(
                src_ref=ref_of(source), dst_ref=ref_of(target), send_sem=send_sem, recv_sem=recv_of(target),
                device_id=(group, my_r), device_id_type=MESH,
            ).start()

    exchange(lambda slot: geo.at[slot], geo_send, lambda slot: geo_recv.at[slot])
    exchange(lambda slot: halo.at[0, slot], halo_send.at[0], lambda slot: halo_recv.at[0, slot])

    acc[...] = jnp.zeros_like(acc)

    def own_pieces(turn, carry):
        make_tiles(own_group_slot(turn), True)
        return carry

    lax.fori_loop(0, rep_n, own_pieces, 0)
    hear(0)
    tell(1)

    def come_slot(turn):
        return jnp.where(upward(turn), turn, REACH + turn)

    def come_product(slot):
        await_bytes(halo.at[0, slot], halo_recv.at[0, slot])
        add_product(0, slot)

    def other_pieces(turn, carry):
        slot = come_slot(turn)
        await_bytes(geo.at[slot], geo_recv.at[slot])
        come_product(come_slot(turn - 1))
        make_tiles(slot, False)
        return carry

    await_bytes(geo.at[0], geo_recv.at[0])
    make_tiles(0, False, (0, width - step_rows))
    lax.fori_loop(1, rep_n, other_pieces, 0)
    await_bytes(geo.at[2 * REACH], geo_recv.at[2 * REACH])
    come_product(come_slot(rep_n - 1))
    make_tiles(2 * REACH, False, (width - step_rows, 0))
    come_product(2 * REACH)
    hear(1)
    tell(2)
    def spread_halo(stage):
        for offset in OFFSETS:
            pltpu.make_async_remote_copy(
                src_ref=halo.at[stage, REACH], dst_ref=halo.at[stage, REACH - offset],
                send_sem=halo_send.at[stage], recv_sem=halo_recv.at[stage, REACH - offset],
                device_id=chain_device(offset), device_id_type=MESH,
            ).start()

    def add_side(stage, offsets):
        for offset in offsets:
            slot = REACH - offset
            await_bytes(halo.at[stage, slot], halo_recv.at[stage, slot])
            add_product(stage, slot)

    def folded(first, second):
        value = first * second
        total = value[:, :128]
        for at in range(128, width, 128):
            total = total + value[:, at:at + 128]
        return total

    def as_row(pieces):
        return jnp.sum(jnp.transpose(jnp.concatenate(pieces, axis=0)), axis=0, keepdims=True)

    def columns_of(row):
        return jnp.transpose(jnp.concatenate([row, jnp.zeros((8 - row.shape[0], 128), F32)], axis=0))

    def begin_sum(slots, send_sem, recv_sem):
        for step in range(1, n1):
            pltpu.make_async_remote_copy(
                src_ref=slots.at[place1], dst_ref=slots.at[place1], send_sem=send_sem, recv_sem=recv_sem,
                device_id=device1(step), device_id_type=MESH,
            ).start()

    def pass_sum(slots, recv_sem, slots_next, send_sem_next, recv_sem_next):
        await_bytes(slots.at[pl.ds(0, n1 - 1)], recv_sem)
        slots_next[place2] = jnp.sum(slots[...], axis=0)
        for step in range(1, n2):
            pltpu.make_async_remote_copy(
                src_ref=slots_next.at[place2], dst_ref=slots_next.at[place2],
                send_sem=send_sem_next, recv_sem=recv_sem_next,
                device_id=device2(step), device_id_type=MESH,
            ).start()

    def end_sum(slots, recv_sem):
        await_bytes(slots.at[pl.ds(0, n2 - 1)], recv_sem)
        return columns_of(jnp.sum(slots[...], axis=0))

    halo[1, REACH] = image_of(0)
    spread_halo(1)
    acc[...] = jnp.zeros_like(acc)
    add_product(1, REACH)
    start, first = halo[0, REACH], halo[1, REACH]
    sums1[place1] = as_row([
        folded(start, start), folded(start, first), folded(first, first), jnp.zeros((128 - 3 * months, 128), F32)
    ])
    hear(2)
    tell(3)
    begin_sum(sums1, sum_send.at[0], sum_recv.at[0])
    add_side(1, AHEAD)
    hear(3)
    tell(4)
    add_side(1, BEHIND)
    halo[2, REACH] = image_of(1)
    spread_halo(2)
    hear(4)
    pass_sum(sums1, sum_recv.at[0], sums2, sum_send.at[1], sum_recv.at[1])
    second = halo[2, REACH]
    known = [folded(halo[1, REACH], second), folded(second, second)]
    acc[...] = jnp.zeros_like(acc)
    add_product(2, REACH)
    within = acc[...]
    add_side(2, AHEAD)
    doubled = own_scale * (2.0 * acc[...] - within) + own_nugget * halo[2, REACH]
    pair[my_core] = as_row(
        known + [folded(halo[2, REACH], doubled), jnp.zeros((128 - 3 * months, 128), F32)]
    )
    pair_copy = pltpu.make_async_remote_copy(
        src_ref=pair.at[my_core], dst_ref=pair.at[my_core], send_sem=pair_sems.at[0], recv_sem=pair_sems.at[1],
        device_id=(my_s + 1 - 2 * my_core, my_r), device_id_type=MESH,
    )
    pair_copy.start()
    await_bytes(pair.at[0], pair_sems.at[1])
    late[chip] = pair[0] + pair[1]
    for ahead_z in swing(z_n):
        for ahead_y in swing(y_n):
            row = ((my_z + ahead_z) % z_n) * y_n + (my_y + ahead_y) % y_n
            for ahead_r in swing(rep_n):
                if ahead_z or ahead_y or ahead_r:
                    pltpu.make_async_remote_copy(
                        src_ref=late.at[chip], dst_ref=late.at[chip],
                        send_sem=sum_send.at[2], recv_sem=sum_recv.at[2],
                        device_id=(row * 2 + my_core, (my_r + ahead_r) % rep_n), device_id_type=MESH,
                    ).start()
    add_side(2, BEHIND)
    last[my_r] = image_of(2)
    for step in range(1, rep_n):
        pltpu.make_async_remote_copy(
            src_ref=last.at[my_r], dst_ref=last.at[my_r],
            send_sem=last_send, recv_sem=last_recv.at[step],
            device_id=(my_s, (my_r + step) % rep_n), device_id_type=MESH,
        ).start()

    def thirds(columns):
        return [columns[at * months:(at + 1) * months, 0:1] for at in range(3)]

    m0, m1, m2 = thirds(end_sum(sums2, sum_recv.at[1]))
    alpha0 = m0 / m1
    norm1 = alpha0 * alpha0 * m2 - m0
    lead = 1.0 + norm1 / m0
    for step in range(1, rep_n):
        await_bytes(last.at[0], last_recv.at[step])
    count = len(OFFSETS)
    await_bytes(geo.at[pl.ds(0, rep_n + 1)], geo_send)
    await_bytes(halo.at[0, pl.ds(0, rep_n + 1)], halo_send.at[0])
    for stage in range(1, 3):
        await_bytes(halo.at[stage, pl.ds(0, count)], halo_send.at[stage])
    await_bytes(last.at[pl.ds(0, rep_n - 1)], last_send)
    await_bytes(sums1.at[pl.ds(0, n1 - 1)], sum_send.at[0])
    await_bytes(sums2.at[pl.ds(0, n2 - 1)], sum_send.at[1])

    await_bytes(late.at[pl.ds(0, chain_n // 2 - 1)], sum_recv.at[2])
    m3, m4, m5 = thirds(columns_of(jnp.sum(late[...], axis=0)))
    alpha1 = norm1 / (alpha0 * (alpha0 * m3 - lead * m2))
    r1 = -(alpha0 + alpha1 * lead)
    r2 = alpha0 * alpha1
    norm2 = r2 * (m2 + r1 * m3 + r2 * m4)
    beta2 = norm2 / norm1
    d0 = 1.0 + beta2 * lead
    d1 = r1 - beta2 * alpha0
    alpha2 = norm2 / (r2 * (d0 * m3 + d1 * m4 + r2 * m5))
    found = (alpha2 * d0 - r1, alpha2 * d1 - r2, alpha2 * r2)
    left = (r1 - alpha2 * d0, r2 - alpha2 * d1, -alpha2 * r2)
    for place in range(rep_n):
        lanes = slice(place * width, (place + 1) * width)
        slot = REACH + place - my_r
        start, first, second = halo[0, slot], halo[1, slot], halo[2, slot]
        out_solution[:, lanes] = found[0] * start + found[1] * first + found[2] * second
        out_residual[:, lanes] = start + left[0] * first + left[1] * second + left[2] * last[place]
    await_bytes(late.at[pl.ds(0, chain_n // 2 - 1)], sum_send.at[2])
    await_bytes(pair.at[0], pair_sems.at[0])


def solution(mesh):
    sites_n, rep_n = mesh.shape["sites"], mesh.shape["rep"]
    y_n = 4
    z_n = sites_n // (2 * y_n)

    def local(coords, scale, nugget, right_side, site_order, pair_list, pair_count):
        months, group_width = right_side.shape
        width = group_width // rep_n
        anywhere = pl.BlockSpec(memory_space=pl.ANY)
        dma = pltpu.SemaphoreType.DMA
        out = jax.ShapeDtypeStruct((months, group_width), F32)
        return pl.pallas_call(
            functools.partial(kernel, (sites_n, rep_n, z_n, y_n)),
            out_shape=(out, out),
            in_specs=[anywhere] * 5,
            out_specs=(pl.BlockSpec(memory_space=pltpu.VMEM),) * 2,
            scratch_shapes=[
                pltpu.VMEM((2, group_width), F32),
                pltpu.VMEM((1, group_width), F32),
                pltpu.VMEM((1, group_width), F32),
                pltpu.VMEM((months, group_width), F32),
                pltpu.VMEM((1, group_width), jnp.int32),
                pltpu.VMEM((3 * months + 32, group_width), BF16),
                pltpu.VMEM((SLOTS, width, width), BF16),
                pltpu.VMEM((SLOTS, width, width), BF16),
                pltpu.VMEM((SLOTS, 8, width), F32),
                pltpu.VMEM((3, SLOTS, months, width), F32),
                pltpu.VMEM((rep_n, months, width), F32),
                pltpu.VMEM((months, width), F32),
                pltpu.VMEM((rep_n * y_n, 1, 128), F32),
                pltpu.VMEM((2 * z_n, 1, 128), F32),
                pltpu.VMEM((sites_n * rep_n // 2, 1, 128), F32),
                pltpu.VMEM((2, 1, 128), F32),
                dma((5,)), dma, dma((SLOTS,)), dma((3,)), dma((3, SLOTS)), dma, dma((rep_n,)),
                dma((3,)), dma((3,)), dma((2,)), pltpu.SemaphoreType.REGULAR((5,)),
            ],
            compiler_params=pltpu.CompilerParams(
                collective_id=0, has_side_effects=True, vmem_limit_bytes=56 * 2**20
            ),
        )(coords, scale[None, :], nugget[None, :], right_side, site_order[None, :])

    in_specs = (
        P(None, "sites"),
        P("sites"),
        P("sites"),
        P(None, "sites"),
        P("sites"),
        P(None, ("sites", "rep")),
        P(("sites", "rep")),
    )
    out_specs = (P(None, "sites"), P(None, "sites"))
    return jax.shard_map(local, mesh=mesh, in_specs=in_specs, out_specs=out_specs, check_vma=False)
```

```python
import functools

import jax
import jax.numpy as jnp
from jax import lax
from jax.experimental import pallas as pl
from jax.experimental.pallas import tpu as pltpu
from jax.sharding import PartitionSpec as P

MESH = pl.DeviceIdType.MESH
RANGE_KM = 200.0
TAPER_UNIT = 4.0 / RANGE_KM**5
F32 = jnp.float32
BF16 = jnp.bfloat16
REACH = 4
SLOTS = 2 * REACH + 1
AHEAD = (-2, -3, -1, -4)
BEHIND = (2, 3, 1, 4)
OFFSETS = AHEAD + BEHIND


def split3(value):
    high = value.astype(BF16).astype(F32)
    rest = value - high
    middle = rest.astype(BF16).astype(F32)
    return high, middle, rest - middle


def swing(count):
    return sorted(range(count), key=lambda ahead: -min(ahead, count - ahead))


def kernel(
    sizes,
    coords_in, scale_in, nugget_in, right_side_in, order_in,
    out,
    coords, scale, nugget, right_side, order,
    data, tile_high, tile_low, geo, halo, last, acc, sums1, sums2, late, pair,
    in_sems, geo_send, geo_recv, halo_send, halo_recv, last_send, last_recv,
    sum_send, sum_recv, pair_sems, told,
):
    sites_n, rep_n, z_n, y_n = sizes
    months, group_width = right_side.shape
    width = group_width // rep_n
    chain_n = sites_n * rep_n
    my_s = lax.axis_index("sites")
    my_r = lax.axis_index("rep")
    chain = my_s * rep_n + my_r
    my_core = my_s % 2
    my_y = (my_s // 2) % y_n
    my_z = my_s // (2 * y_n)
    n1 = rep_n * y_n
    n2 = 2 * z_n
    place1 = my_r * y_n + my_y
    place2 = my_z * 2 + my_core
    chip = (my_s // 2) * rep_n + my_r

    def chain_device(offset):
        other = (chain + offset + chain_n) % chain_n
        return (other // rep_n, other % rep_n)

    def device1(step):
        other = (place1 + step) % n1
        return ((my_z * y_n + other % y_n) * 2 + my_core, other // y_n)

    def device2(step):
        other = (place2 + step) % n2
        return (((other // 2) * y_n + my_y) * 2 + other % 2, my_r)

    barrier = pltpu.get_barrier_semaphore()
    peers = (
        [chain_device(REACH), chain_device(-REACH)]
        + [(my_s, (my_r + step) % rep_n) for step in range(1, rep_n)]
    )
    for peer in peers:
        pl.semaphore_signal(barrier, inc=1, device_id=peer, device_id_type=MESH)

    loads = [
        pltpu.make_async_copy(source, target, in_sems.at[at])
        for at, (source, target) in enumerate((
            (right_side_in, right_side), (coords_in, coords), (scale_in, scale),
            (nugget_in, nugget), (order_in, order),
        ))
    ]
    for load in loads:
        load.start()
    for load in loads:
        load.wait()

    def tell(step):
        for group in (my_s + 2**step, my_s + sites_n - 2**step):
            pl.semaphore_signal(
                told.at[step], inc=1, device_id=(group % sites_n, my_r), device_id_type=MESH
            )

    def hear(step):
        pl.semaphore_wait(told.at[step], 2)

    def await_bytes(ref, sem):
        pltpu.make_async_copy(ref, ref, sem).wait()

    site = jnp.concatenate(
        [coords[...], scale[...], nugget[...], jnp.zeros((4, group_width), F32)], axis=0
    )
    for at, part in enumerate(split3(right_side[...])):
        data[at * months:(at + 1) * months, :] = part.astype(BF16)
    parts = split3(site)
    top = 3 * months
    data[top:top + 16, :] = jnp.concatenate(parts[:2], axis=0).astype(BF16)
    data[top + 16:top + 32, :] = jnp.concatenate(
        [parts[2], jnp.zeros((8, group_width), F32)], axis=0
    ).astype(BF16)
    step_rows = 256
    rows_at = lax.broadcasted_iota(jnp.int32, (step_rows, width), 0)

    def own_group_slot(turn):
        return REACH - my_r + (my_r + turn) % rep_n

    def place_sites(turn, carry):
        slot = own_group_slot(turn)
        start = pl.multiple_of(((my_r + turn) % rep_n) * width, width)
        wanted = order[:, pl.ds(start, width)] - my_s * group_width
        placed = jnp.zeros((top + 32, width), F32)
        for at in range(group_width // step_rows):
            chosen = jnp.where(rows_at == wanted - at * step_rows, 1.0, 0.0).astype(BF16)
            placed = placed + jnp.dot(
                data[:, at * step_rows:(at + 1) * step_rows], chosen, preferred_element_type=F32
            )
        halo[0, slot] = (placed[:months] + placed[months:2 * months]) + placed[2 * months:top]
        geo[slot] = (placed[top:top + 8] + placed[top + 8:top + 16]) + placed[top + 16:top + 24]
        return carry

    lax.fori_loop(0, rep_n, place_sites, 0)
    own_geo = geo[REACH]
    own_scale = own_geo[2:3] * TAPER_UNIT
    own_nugget = own_geo[3:4]

    def split2(vector):
        high = vector.astype(BF16)
        return high, (vector - high.astype(F32)).astype(BF16)

    def parts_of(stage, slot):
        high, low = split2(halo[stage, slot] * geo[slot][2:3])
        return jnp.concatenate([high, low], axis=0), high

    def tile_product(both, high, tiles, rest):
        large = jnp.dot(both, tiles, preferred_element_type=F32)
        small = jnp.dot(high, rest, preferred_element_type=F32)
        return large[:months] + (large[months:] + small)

    def add_product(stage, slot):
        both, high = parts_of(stage, slot)
        acc[...] += tile_product(both, high, tile_high[slot], tile_low[slot])

    def make_tiles(slot, use, out_of_reach=None):
        away = (chain + slot - REACH < 0) | (chain + slot - REACH >= chain_n)
        shift = jnp.where(away, 1.0e6, 0.0).astype(F32)
        columns = jnp.transpose(geo[slot])
        if use:
            both, first = parts_of(0, slot)
        total = jnp.zeros((months, width), F32)
        for at in range(0, width, step_rows):
            lanes = slice(0, width)
            if out_of_reach and out_of_reach[0] == at:
                lanes = slice(0, out_of_reach[1]) if out_of_reach[1] else slice(step_rows, width)
            east = columns[at:at + step_rows, 0:1] + shift
            north = columns[at:at + step_rows, 1:2]
            d_east = east - own_geo[0:1, lanes]
            d_north = north - own_geo[1:2, lanes]
            squared = jnp.clip(d_east * d_east + d_north * d_north, 1.0e-30, RANGE_KM * RANGE_KM)
            distance = squared * lax.rsqrt(squared)
            remain = RANGE_KM - distance
            square = remain * remain
            high, low = split2((square * square) * (distance + 0.25 * RANGE_KM))
            if out_of_reach and out_of_reach[0] == at:
                blank = slice(out_of_reach[1], out_of_reach[1] + step_rows)
                tile_high[slot, at:at + step_rows, blank] = jnp.zeros((step_rows, step_rows), BF16)
                tile_low[slot, at:at + step_rows, blank] = jnp.zeros((step_rows, step_rows), BF16)
            tile_high[slot, at:at + step_rows, lanes] = high
            tile_low[slot, at:at + step_rows, lanes] = low
            if use:
                total = total + tile_product(
                    both[:, at:at + step_rows], first[:, at:at + step_rows], high, low
                )
        if use:
            acc[...] += total

    def image_of(stage):
        return own_scale * acc[...] + own_nugget * halo[stage, REACH]

    pl.semaphore_wait(barrier, len(peers))
    tell(0)

    def upward(turn):
        return turn <= rep_n - 1 - my_r

    def exchange(ref_of, send_sem, recv_of):
        for turn in range(rep_n + 1):
            up = upward(turn)
            source = jnp.where(up, REACH + turn, turn)
            target = jnp.where(up, turn, REACH + turn)
            group = (my_s + jnp.where(up, 1, sites_n - 1)) % sites_n
            pltpu.make_async_remote_copy(
                src_ref=ref_of(source), dst_ref=ref_of(target), send_sem=send_sem, recv_sem=recv_of(target),
                device_id=(group, my_r), device_id_type=MESH,
            ).start()

    exchange(lambda slot: geo.at[slot], geo_send, lambda slot: geo_recv.at[slot])
    exchange(lambda slot: halo.at[0, slot], halo_send.at[0], lambda slot: halo_recv.at[0, slot])

    acc[...] = jnp.zeros_like(acc)

    def own_pieces(turn, carry):
        make_tiles(own_group_slot(turn), True)
        return carry

    lax.fori_loop(0, rep_n, own_pieces, 0)
    hear(0)
    tell(1)

    def come_slot(turn):
        return jnp.where(upward(turn), turn, REACH + turn)

    def come_product(slot):
        await_bytes(halo.at[0, slot], halo_recv.at[0, slot])
        add_product(0, slot)

    def other_pieces(turn, carry):
        slot = come_slot(turn)
        await_bytes(geo.at[slot], geo_recv.at[slot])
        come_product(come_slot(turn - 1))
        make_tiles(slot, False)
        return carry

    await_bytes(geo.at[0], geo_recv.at[0])
    make_tiles(0, False, (0, width - step_rows))
    lax.fori_loop(1, rep_n, other_pieces, 0)
    await_bytes(geo.at[2 * REACH], geo_recv.at[2 * REACH])
    come_product(come_slot(rep_n - 1))
    make_tiles(2 * REACH, False, (width - step_rows, 0))
    come_product(2 * REACH)
    hear(1)
    tell(2)
    def spread_halo(stage):
        for offset in OFFSETS:
            pltpu.make_async_remote_copy(
                src_ref=halo.at[stage, REACH], dst_ref=halo.at[stage, REACH - offset],
                send_sem=halo_send.at[stage], recv_sem=halo_recv.at[stage, REACH - offset],
                device_id=chain_device(offset), device_id_type=MESH,
            ).start()

    def add_side(stage, offsets):
        for offset in offsets:
            slot = REACH - offset
            await_bytes(halo.at[stage, slot], halo_recv.at[stage, slot])
            add_product(stage, slot)

    def folded(first, second):
        value = first * second
        total = value[:, :128]
        for at in range(128, width, 128):
            total = total + value[:, at:at + 128]
        return total

    def as_row(pieces):
        return jnp.sum(jnp.transpose(jnp.concatenate(pieces, axis=0)), axis=0, keepdims=True)

    def columns_of(row):
        return jnp.transpose(jnp.concatenate([row, jnp.zeros((8 - row.shape[0], 128), F32)], axis=0))

    def begin_sum(slots, send_sem, recv_sem):
        for step in range(1, n1):
            pltpu.make_async_remote_copy(
                src_ref=slots.at[place1], dst_ref=slots.at[place1], send_sem=send_sem, recv_sem=recv_sem,
                device_id=device1(step), device_id_type=MESH,
            ).start()

    def pass_sum(slots, recv_sem, slots_next, send_sem_next, recv_sem_next):
        await_bytes(slots.at[pl.ds(0, n1 - 1)], recv_sem)
        slots_next[place2] = jnp.sum(slots[...], axis=0)
        for step in range(1, n2):
            pltpu.make_async_remote_copy(
                src_ref=slots_next.at[place2], dst_ref=slots_next.at[place2],
                send_sem=send_sem_next, recv_sem=recv_sem_next,
                device_id=device2(step), device_id_type=MESH,
            ).start()

    def end_sum(slots, recv_sem):
        await_bytes(slots.at[pl.ds(0, n2 - 1)], recv_sem)
        return columns_of(jnp.sum(slots[...], axis=0))

    halo[1, REACH] = image_of(0)
    spread_halo(1)
    acc[...] = jnp.zeros_like(acc)
    add_product(1, REACH)
    start, first = halo[0, REACH], halo[1, REACH]
    sums1[place1] = as_row([
        folded(start, start), folded(start, first), folded(first, first), jnp.zeros((128 - 3 * months, 128), F32)
    ])
    hear(2)
    tell(3)
    begin_sum(sums1, sum_send.at[0], sum_recv.at[0])
    add_side(1, AHEAD)
    hear(3)
    tell(4)
    add_side(1, BEHIND)
    halo[2, REACH] = image_of(1)
    spread_halo(2)
    hear(4)
    pass_sum(sums1, sum_recv.at[0], sums2, sum_send.at[1], sum_recv.at[1])
    second = halo[2, REACH]
    known = [folded(halo[1, REACH], second), folded(second, second)]
    acc[...] = jnp.zeros_like(acc)
    add_product(2, REACH)
    within = acc[...]
    add_side(2, AHEAD)
    doubled = own_scale * (2.0 * acc[...] - within) + own_nugget * halo[2, REACH]
    pair[my_core] = as_row(
        known + [folded(halo[2, REACH], doubled), jnp.zeros((128 - 3 * months, 128), F32)]
    )
    pair_copy = pltpu.make_async_remote_copy(
        src_ref=pair.at[my_core], dst_ref=pair.at[my_core], send_sem=pair_sems.at[0], recv_sem=pair_sems.at[1],
        device_id=(my_s + 1 - 2 * my_core, my_r), device_id_type=MESH,
    )
    pair_copy.start()
    await_bytes(pair.at[0], pair_sems.at[1])
    late[chip] = pair[0] + pair[1]
    for ahead_z in swing(z_n):
        for ahead_y in swing(y_n):
            row = ((my_z + ahead_z) % z_n) * y_n + (my_y + ahead_y) % y_n
            for ahead_r in swing(rep_n):
                if ahead_z or ahead_y or ahead_r:
                    pltpu.make_async_remote_copy(
                        src_ref=late.at[chip], dst_ref=late.at[chip],
                        send_sem=sum_send.at[2], recv_sem=sum_recv.at[2],
                        device_id=(row * 2 + my_core, (my_r + ahead_r) % rep_n), device_id_type=MESH,
                    ).start()
    add_side(2, BEHIND)
    last[my_r] = image_of(2)
    for step in range(1, rep_n):
        pltpu.make_async_remote_copy(
            src_ref=last.at[my_r], dst_ref=last.at[my_r],
            send_sem=last_send, recv_sem=last_recv.at[step],
            device_id=(my_s, (my_r + step) % rep_n), device_id_type=MESH,
        ).start()

    def thirds(columns):
        return [columns[at * months:(at + 1) * months, 0:1] for at in range(3)]

    m0, m1, m2 = thirds(end_sum(sums2, sum_recv.at[1]))
    alpha0 = m0 / m1
    norm1 = alpha0 * alpha0 * m2 - m0
    lead = 1.0 + norm1 / m0
    for step in range(1, rep_n):
        await_bytes(last.at[0], last_recv.at[step])
    count = len(OFFSETS)
    await_bytes(geo.at[pl.ds(0, rep_n + 1)], geo_send)
    await_bytes(halo.at[0, pl.ds(0, rep_n + 1)], halo_send.at[0])
    for stage in range(1, 3):
        await_bytes(halo.at[stage, pl.ds(0, count)], halo_send.at[stage])
    await_bytes(last.at[pl.ds(0, rep_n - 1)], last_send)
    await_bytes(sums1.at[pl.ds(0, n1 - 1)], sum_send.at[0])
    await_bytes(sums2.at[pl.ds(0, n2 - 1)], sum_send.at[1])

    await_bytes(late.at[pl.ds(0, chain_n // 2 - 1)], sum_recv.at[2])
    m3, m4, m5 = thirds(columns_of(jnp.sum(late[...], axis=0)))
    alpha1 = norm1 / (alpha0 * (alpha0 * m3 - lead * m2))
    r1 = -(alpha0 + alpha1 * lead)
    r2 = alpha0 * alpha1
    norm2 = r2 * (m2 + r1 * m3 + r2 * m4)
    beta2 = norm2 / norm1
    d0 = 1.0 + beta2 * lead
    d1 = r1 - beta2 * alpha0
    alpha2 = norm2 / (r2 * (d0 * m3 + d1 * m4 + r2 * m5))
    found = (alpha2 * d0 - r1, alpha2 * d1 - r2, alpha2 * r2)
    left = (r1 - alpha2 * d0, r2 - alpha2 * d1, -alpha2 * r2)
    for place in range(rep_n):
        lanes = slice(place * width, (place + 1) * width)
        slot = REACH + place - my_r
        start, first, second = halo[0, slot], halo[1, slot], halo[2, slot]
        out[0, :, lanes] = found[0] * start + found[1] * first + found[2] * second
        out[1, :, lanes] = start + left[0] * first + left[1] * second + left[2] * last[place]
    await_bytes(late.at[pl.ds(0, chain_n // 2 - 1)], sum_send.at[2])
    await_bytes(pair.at[0], pair_sems.at[0])


def solution(mesh):
    sites_n, rep_n = mesh.shape["sites"], mesh.shape["rep"]
    y_n = 4
    z_n = sites_n // (2 * y_n)

    def local(coords, scale, nugget, right_side, site_order, pair_list, pair_count):
        months, group_width = right_side.shape
        width = group_width // rep_n
        anywhere = pl.BlockSpec(memory_space=pl.ANY)
        dma = pltpu.SemaphoreType.DMA
        both = pl.pallas_call(
            functools.partial(kernel, (sites_n, rep_n, z_n, y_n)),
            out_shape=jax.ShapeDtypeStruct((2, months, group_width), F32),
            in_specs=[anywhere] * 5,
            out_specs=pl.BlockSpec(memory_space=pltpu.VMEM),
            scratch_shapes=[
                pltpu.VMEM((2, group_width), F32),
                pltpu.VMEM((1, group_width), F32),
                pltpu.VMEM((1, group_width), F32),
                pltpu.VMEM((months, group_width), F32),
                pltpu.VMEM((1, group_width), jnp.int32),
                pltpu.VMEM((3 * months + 32, group_width), BF16),
                pltpu.VMEM((SLOTS, width, width), BF16),
                pltpu.VMEM((SLOTS, width, width), BF16),
                pltpu.VMEM((SLOTS, 8, width), F32),
                pltpu.VMEM((3, SLOTS, months, width), F32),
                pltpu.VMEM((rep_n, months, width), F32),
                pltpu.VMEM((months, width), F32),
                pltpu.VMEM((rep_n * y_n, 1, 128), F32),
                pltpu.VMEM((2 * z_n, 1, 128), F32),
                pltpu.VMEM((sites_n * rep_n // 2, 1, 128), F32),
                pltpu.VMEM((2, 1, 128), F32),
                dma((5,)), dma, dma((SLOTS,)), dma((3,)), dma((3, SLOTS)), dma, dma((rep_n,)),
                dma((3,)), dma((3,)), dma((2,)), pltpu.SemaphoreType.REGULAR((5,)),
            ],
            compiler_params=pltpu.CompilerParams(
                collective_id=0, has_side_effects=True, vmem_limit_bytes=56 * 2**20
            ),
        )(coords, scale[None, :], nugget[None, :], right_side, site_order[None, :])
        return (both[0], both[1])

    in_specs = (
        P(None, "sites"),
        P("sites"),
        P("sites"),
        P(None, "sites"),
        P("sites"),
        P(None, ("sites", "rep")),
        P(("sites", "rep")),
    )
    out_specs = (P(None, "sites"), P(None, "sites"))
    return jax.shard_map(local, mesh=mesh, in_specs=in_specs, out_specs=out_specs, check_vma=False)
```

```python
import functools

import jax
import jax.numpy as jnp
from jax import lax
from jax.experimental import pallas as pl
from jax.experimental.pallas import tpu as pltpu
from jax.sharding import PartitionSpec as P

MESH = pl.DeviceIdType.MESH
RANGE_KM = 200.0
TAPER_UNIT = 4.0 / RANGE_KM**5
F32 = jnp.float32
BF16 = jnp.bfloat16
REACH = 4
SLOTS = 2 * REACH + 1
AHEAD = (-2, -3, -1, -4)
BEHIND = (2, 3, 1, 4)
OFFSETS = AHEAD + BEHIND


def split3(value):
    high = value.astype(BF16).astype(F32)
    rest = value - high
    middle = rest.astype(BF16).astype(F32)
    return high, middle, rest - middle


def swing(count):
    return sorted(range(count), key=lambda ahead: -min(ahead, count - ahead))


def kernel(
    sizes,
    coords_in, scale_in, nugget_in, right_side_in, order_in,
    out,
    coords, scale, nugget, right_side, order,
    data, tile_high, tile_low, geo, halo, last, acc, sums1, sums2, late, pair,
    in_sems, geo_send, geo_recv, halo_send, halo_recv, last_send, last_recv,
    sum_send, sum_recv, pair_sems, told,
):
    sites_n, rep_n, z_n, y_n = sizes
    months, group_width = right_side.shape
    width = group_width // rep_n
    chain_n = sites_n * rep_n
    my_s = lax.axis_index("sites")
    my_r = lax.axis_index("rep")
    chain = my_s * rep_n + my_r
    my_core = my_s % 2
    my_y = (my_s // 2) % y_n
    my_z = my_s // (2 * y_n)
    n1 = rep_n * y_n
    n2 = 2 * z_n
    place1 = my_r * y_n + my_y
    place2 = my_z * 2 + my_core
    chip = (my_s // 2) * rep_n + my_r

    def chain_device(offset):
        other = (chain + offset + chain_n) % chain_n
        return (other // rep_n, other % rep_n)

    def device1(step):
        other = (place1 + step) % n1
        return ((my_z * y_n + other % y_n) * 2 + my_core, other // y_n)

    def device2(step):
        other = (place2 + step) % n2
        return (((other // 2) * y_n + my_y) * 2 + other % 2, my_r)

    barrier = pltpu.get_barrier_semaphore()
    peers = (
        [chain_device(REACH), chain_device(-REACH)]
        + [(my_s, (my_r + step) % rep_n) for step in range(1, rep_n)]
    )
    for peer in peers:
        pl.semaphore_signal(barrier, inc=1, device_id=peer, device_id_type=MESH)

    loads = [
        pltpu.make_async_copy(source, target, in_sems.at[at])
        for at, (source, target) in enumerate((
            (right_side_in, right_side), (coords_in, coords), (scale_in, scale),
            (nugget_in, nugget), (order_in, order),
        ))
    ]
    for load in loads:
        load.start()
    for load in loads:
        load.wait()

    def tell(step):
        for group in (my_s + 2**step, my_s + sites_n - 2**step):
            pl.semaphore_signal(
                told.at[step], inc=1, device_id=(group % sites_n, my_r), device_id_type=MESH
            )

    def hear(step):
        pl.semaphore_wait(told.at[step], 2)

    def await_bytes(ref, sem):
        pltpu.make_async_copy(ref, ref, sem).wait()

    site = jnp.concatenate(
        [coords[...], scale[...], nugget[...], jnp.zeros((4, group_width), F32)], axis=0
    )
    for at, part in enumerate(split3(right_side[...])):
        data[at * months:(at + 1) * months, :] = part.astype(BF16)
    parts = split3(site)
    top = 3 * months
    data[top:top + 16, :] = jnp.concatenate(parts[:2], axis=0).astype(BF16)
    data[top + 16:top + 32, :] = jnp.concatenate(
        [parts[2], jnp.zeros((8, group_width), F32)], axis=0
    ).astype(BF16)
    step_rows = 256
    rows_at = lax.broadcasted_iota(jnp.int32, (step_rows, width), 0)

    def own_group_slot(turn):
        return REACH - my_r + (my_r + turn) % rep_n

    def place_sites(turn, carry):
        slot = own_group_slot(turn)
        start = pl.multiple_of(((my_r + turn) % rep_n) * width, width)
        wanted = order[:, pl.ds(start, width)] - my_s * group_width
        placed = jnp.zeros((top + 32, width), F32)
        for at in range(group_width // step_rows):
            chosen = jnp.where(rows_at == wanted - at * step_rows, 1.0, 0.0).astype(BF16)
            placed = placed + jnp.dot(
                data[:, at * step_rows:(at + 1) * step_rows], chosen, preferred_element_type=F32
            )
        halo[0, slot] = (placed[:months] + placed[months:2 * months]) + placed[2 * months:top]
        geo[slot] = (placed[top:top + 8] + placed[top + 8:top + 16]) + placed[top + 16:top + 24]
        return carry

    lax.fori_loop(0, rep_n, place_sites, 0)
    own_geo = geo[REACH]
    own_scale = own_geo[2:3] * TAPER_UNIT
    own_nugget = own_geo[3:4]

    def split2(vector):
        high = vector.astype(BF16)
        return high, (vector - high.astype(F32)).astype(BF16)

    def parts_of(stage, slot):
        high, low = split2(halo[stage, slot] * geo[slot][2:3])
        return jnp.concatenate([high, low], axis=0), high

    def tile_product(both, high, tiles, rest):
        large = jnp.dot(both, tiles, preferred_element_type=F32)
        small = jnp.dot(high, rest, preferred_element_type=F32)
        return large[:months] + (large[months:] + small)

    def add_product(stage, slot):
        both, high = parts_of(stage, slot)
        acc[...] += tile_product(both, high, tile_high[slot], tile_low[slot])

    def make_tiles(slot, use, out_of_reach=None):
        away = (chain + slot - REACH < 0) | (chain + slot - REACH >= chain_n)
        shift = jnp.where(away, 1.0e6, 0.0).astype(F32)
        columns = jnp.transpose(geo[slot])
        if use:
            both, first = parts_of(0, slot)
        total = jnp.zeros((months, width), F32)
        for at in range(0, width, step_rows):
            lanes = slice(0, width)
            if out_of_reach and out_of_reach[0] == at:
                lanes = slice(0, out_of_reach[1]) if out_of_reach[1] else slice(step_rows, width)
            east = columns[at:at + step_rows, 0:1] + shift
            north = columns[at:at + step_rows, 1:2]
            d_east = east - own_geo[0:1, lanes]
            d_north = north - own_geo[1:2, lanes]
            squared = jnp.clip(d_east * d_east + d_north * d_north, 1.0e-30, RANGE_KM * RANGE_KM)
            distance = squared * lax.rsqrt(squared)
            remain = RANGE_KM - distance
            square = remain * remain
            high, low = split2((square * square) * (distance + 0.25 * RANGE_KM))
            if out_of_reach and out_of_reach[0] == at:
                blank = slice(out_of_reach[1], out_of_reach[1] + step_rows)
                tile_high[slot, at:at + step_rows, blank] = jnp.zeros((step_rows, step_rows), BF16)
                tile_low[slot, at:at + step_rows, blank] = jnp.zeros((step_rows, step_rows), BF16)
            tile_high[slot, at:at + step_rows, lanes] = high
            tile_low[slot, at:at + step_rows, lanes] = low
            if use:
                total = total + tile_product(
                    both[:, at:at + step_rows], first[:, at:at + step_rows], high, low
                )
        if use:
            acc[...] += total

    def image_of(stage):
        return own_scale * acc[...] + own_nugget * halo[stage, REACH]

    pl.semaphore_wait(barrier, len(peers))
    tell(0)

    def upward(turn):
        return turn <= rep_n - 1 - my_r

    def exchange(turn, ref_of, send_sem, recv_of):
        up = upward(turn)
        source = jnp.where(up, REACH + turn, turn)
        target = jnp.where(up, turn, REACH + turn)
        group = (my_s + jnp.where(up, 1, sites_n - 1)) % sites_n
        pltpu.make_async_remote_copy(
            src_ref=ref_of(source), dst_ref=ref_of(target), send_sem=send_sem, recv_sem=recv_of(target),
            device_id=(group, my_r), device_id_type=MESH,
        ).start()

    for turn in range(rep_n + 2):
        if turn <= rep_n:
            exchange(turn, lambda slot: geo.at[slot], geo_send, lambda slot: geo_recv.at[slot])
        if turn >= 1:
            exchange(turn - 1, lambda slot: halo.at[0, slot], halo_send.at[0], lambda slot: halo_recv.at[0, slot])

    acc[...] = jnp.zeros_like(acc)

    def own_pieces(turn, carry):
        make_tiles(own_group_slot(turn), True)
        return carry

    lax.fori_loop(0, rep_n, own_pieces, 0)
    hear(0)
    tell(1)

    def come_slot(turn):
        return jnp.where(upward(turn), turn, REACH + turn)

    def come_product(slot):
        await_bytes(halo.at[0, slot], halo_recv.at[0, slot])
        add_product(0, slot)

    def other_pieces(turn, carry):
        slot = come_slot(turn)
        await_bytes(geo.at[slot], geo_recv.at[slot])
        come_product(come_slot(turn - 1))
        make_tiles(slot, False)
        return carry

    await_bytes(geo.at[0], geo_recv.at[0])
    make_tiles(0, False, (0, width - step_rows))
    lax.fori_loop(1, rep_n, other_pieces, 0)
    await_bytes(geo.at[2 * REACH], geo_recv.at[2 * REACH])
    come_product(come_slot(rep_n - 1))
    make_tiles(2 * REACH, False, (width - step_rows, 0))
    come_product(2 * REACH)
    hear(1)
    tell(2)
    def spread_halo(stage):
        for offset in OFFSETS:
            pltpu.make_async_remote_copy(
                src_ref=halo.at[stage, REACH], dst_ref=halo.at[stage, REACH - offset],
                send_sem=halo_send.at[stage], recv_sem=halo_recv.at[stage, REACH - offset],
                device_id=chain_device(offset), device_id_type=MESH,
            ).start()

    def add_side(stage, offsets):
        for offset in offsets:
            slot = REACH - offset
            await_bytes(halo.at[stage, slot], halo_recv.at[stage, slot])
            add_product(stage, slot)

    def folded(first, second):
        value = first * second
        total = value[:, :128]
        for at in range(128, width, 128):
            total = total + value[:, at:at + 128]
        return total

    def as_row(pieces):
        return jnp.sum(jnp.transpose(jnp.concatenate(pieces, axis=0)), axis=0, keepdims=True)

    def columns_of(row):
        return jnp.transpose(jnp.concatenate([row, jnp.zeros((8 - row.shape[0], 128), F32)], axis=0))

    def begin_sum(slots, send_sem, recv_sem):
        for step in range(1, n1):
            pltpu.make_async_remote_copy(
                src_ref=slots.at[place1], dst_ref=slots.at[place1], send_sem=send_sem, recv_sem=recv_sem,
                device_id=device1(step), device_id_type=MESH,
            ).start()

    def pass_sum(slots, recv_sem, slots_next, send_sem_next, recv_sem_next):
        await_bytes(slots.at[pl.ds(0, n1 - 1)], recv_sem)
        slots_next[place2] = jnp.sum(slots[...], axis=0)
        for step in range(1, n2):
            pltpu.make_async_remote_copy(
                src_ref=slots_next.at[place2], dst_ref=slots_next.at[place2],
                send_sem=send_sem_next, recv_sem=recv_sem_next,
                device_id=device2(step), device_id_type=MESH,
            ).start()

    def end_sum(slots, recv_sem):
        await_bytes(slots.at[pl.ds(0, n2 - 1)], recv_sem)
        return columns_of(jnp.sum(slots[...], axis=0))

    halo[1, REACH] = image_of(0)
    spread_halo(1)
    acc[...] = jnp.zeros_like(acc)
    add_product(1, REACH)
    start, first = halo[0, REACH], halo[1, REACH]
    sums1[place1] = as_row([
        folded(start, start), folded(start, first), folded(first, first), jnp.zeros((128 - 3 * months, 128), F32)
    ])
    hear(2)
    tell(3)
    begin_sum(sums1, sum_send.at[0], sum_recv.at[0])
    add_side(1, AHEAD)
    hear(3)
    tell(4)
    add_side(1, BEHIND)
    halo[2, REACH] = image_of(1)
    spread_halo(2)
    hear(4)
    pass_sum(sums1, sum_recv.at[0], sums2, sum_send.at[1], sum_recv.at[1])
    second = halo[2, REACH]
    known = [folded(halo[1, REACH], second), folded(second, second)]
    acc[...] = jnp.zeros_like(acc)
    add_product(2, REACH)
    within = acc[...]
    add_side(2, AHEAD)
    doubled = own_scale * (2.0 * acc[...] - within) + own_nugget * halo[2, REACH]
    pair[my_core] = as_row(
        known + [folded(halo[2, REACH], doubled), jnp.zeros((128 - 3 * months, 128), F32)]
    )
    pair_copy = pltpu.make_async_remote_copy(
        src_ref=pair.at[my_core], dst_ref=pair.at[my_core], send_sem=pair_sems.at[0], recv_sem=pair_sems.at[1],
        device_id=(my_s + 1 - 2 * my_core, my_r), device_id_type=MESH,
    )
    pair_copy.start()
    await_bytes(pair.at[0], pair_sems.at[1])
    late[chip] = pair[0] + pair[1]
    for ahead_z in swing(z_n):
        for ahead_y in swing(y_n):
            row = ((my_z + ahead_z) % z_n) * y_n + (my_y + ahead_y) % y_n
            for ahead_r in swing(rep_n):
                if ahead_z or ahead_y or ahead_r:
                    pltpu.make_async_remote_copy(
                        src_ref=late.at[chip], dst_ref=late.at[chip],
                        send_sem=sum_send.at[2], recv_sem=sum_recv.at[2],
                        device_id=(row * 2 + my_core, (my_r + ahead_r) % rep_n), device_id_type=MESH,
                    ).start()
    add_side(2, BEHIND)
    last[my_r] = image_of(2)
    for step in range(1, rep_n):
        pltpu.make_async_remote_copy(
            src_ref=last.at[my_r], dst_ref=last.at[my_r],
            send_sem=last_send, recv_sem=last_recv.at[step],
            device_id=(my_s, (my_r + step) % rep_n), device_id_type=MESH,
        ).start()

    def thirds(columns):
        return [columns[at * months:(at + 1) * months, 0:1] for at in range(3)]

    m0, m1, m2 = thirds(end_sum(sums2, sum_recv.at[1]))
    alpha0 = m0 / m1
    norm1 = alpha0 * alpha0 * m2 - m0
    lead = 1.0 + norm1 / m0
    for step in range(1, rep_n):
        await_bytes(last.at[0], last_recv.at[step])
    count = len(OFFSETS)
    await_bytes(geo.at[pl.ds(0, rep_n + 1)], geo_send)
    await_bytes(halo.at[0, pl.ds(0, rep_n + 1)], halo_send.at[0])
    for stage in range(1, 3):
        await_bytes(halo.at[stage, pl.ds(0, count)], halo_send.at[stage])
    await_bytes(last.at[pl.ds(0, rep_n - 1)], last_send)
    await_bytes(sums1.at[pl.ds(0, n1 - 1)], sum_send.at[0])
    await_bytes(sums2.at[pl.ds(0, n2 - 1)], sum_send.at[1])

    await_bytes(late.at[pl.ds(0, chain_n // 2 - 1)], sum_recv.at[2])
    m3, m4, m5 = thirds(columns_of(jnp.sum(late[...], axis=0)))
    alpha1 = norm1 / (alpha0 * (alpha0 * m3 - lead * m2))
    r1 = -(alpha0 + alpha1 * lead)
    r2 = alpha0 * alpha1
    norm2 = r2 * (m2 + r1 * m3 + r2 * m4)
    beta2 = norm2 / norm1
    d0 = 1.0 + beta2 * lead
    d1 = r1 - beta2 * alpha0
    alpha2 = norm2 / (r2 * (d0 * m3 + d1 * m4 + r2 * m5))
    found = (alpha2 * d0 - r1, alpha2 * d1 - r2, alpha2 * r2)
    left = (r1 - alpha2 * d0, r2 - alpha2 * d1, -alpha2 * r2)
    for place in range(rep_n):
        lanes = slice(place * width, (place + 1) * width)
        slot = REACH + place - my_r
        start, first, second = halo[0, slot], halo[1, slot], halo[2, slot]
        out[0, :, lanes] = found[0] * start + found[1] * first + found[2] * second
        out[1, :, lanes] = start + left[0] * first + left[1] * second + left[2] * last[place]
    await_bytes(late.at[pl.ds(0, chain_n // 2 - 1)], sum_send.at[2])
    await_bytes(pair.at[0], pair_sems.at[0])


def solution(mesh):
    sites_n, rep_n = mesh.shape["sites"], mesh.shape["rep"]
    y_n = 4
    z_n = sites_n // (2 * y_n)

    def local(coords, scale, nugget, right_side, site_order, pair_list, pair_count):
        months, group_width = right_side.shape
        width = group_width // rep_n
        anywhere = pl.BlockSpec(memory_space=pl.ANY)
        dma = pltpu.SemaphoreType.DMA
        both = pl.pallas_call(
            functools.partial(kernel, (sites_n, rep_n, z_n, y_n)),
            out_shape=jax.ShapeDtypeStruct((2, months, group_width), F32),
            in_specs=[anywhere] * 5,
            out_specs=pl.BlockSpec(memory_space=pltpu.VMEM),
            scratch_shapes=[
                pltpu.VMEM((2, group_width), F32),
                pltpu.VMEM((1, group_width), F32),
                pltpu.VMEM((1, group_width), F32),
                pltpu.VMEM((months, group_width), F32),
                pltpu.VMEM((1, group_width), jnp.int32),
                pltpu.VMEM((3 * months + 32, group_width), BF16),
                pltpu.VMEM((SLOTS, width, width), BF16),
                pltpu.VMEM((SLOTS, width, width), BF16),
                pltpu.VMEM((SLOTS, 8, width), F32),
                pltpu.VMEM((3, SLOTS, months, width), F32),
                pltpu.VMEM((rep_n, months, width), F32),
                pltpu.VMEM((months, width), F32),
                pltpu.VMEM((rep_n * y_n, 1, 128), F32),
                pltpu.VMEM((2 * z_n, 1, 128), F32),
                pltpu.VMEM((sites_n * rep_n // 2, 1, 128), F32),
                pltpu.VMEM((2, 1, 128), F32),
                dma((5,)), dma, dma((SLOTS,)), dma((3,)), dma((3, SLOTS)), dma, dma((rep_n,)),
                dma((3,)), dma((3,)), dma((2,)), pltpu.SemaphoreType.REGULAR((5,)),
            ],
            compiler_params=pltpu.CompilerParams(
                collective_id=0, has_side_effects=True, vmem_limit_bytes=56 * 2**20
            ),
        )(coords, scale[None, :], nugget[None, :], right_side, site_order[None, :])
        return (both[0], both[1])

    in_specs = (
        P(None, "sites"),
        P("sites"),
        P("sites"),
        P(None, "sites"),
        P("sites"),
        P(None, ("sites", "rep")),
        P(("sites", "rep")),
    )
    out_specs = (P(None, "sites"), P(None, "sites"))
    return jax.shard_map(local, mesh=mesh, in_specs=in_specs, out_specs=out_specs, check_vma=False)
```
